32 devices in a mesh: scen: 8 (over y, x, core), col: 4 (over z).
Axes of the slice: x: 2, y: 2, z: 4, core: 2. Of those that a mesh axis runs over, the one named last changes fastest.
Arguments:
- private_seeds: float32 [8, 4, 2, 768, 256], P('scen', 'col'), may hold values from -6 to 6
- private_inverse: float32 [8, 4, 2, 768, 768], P('scen', 'col'), as said below
- coupling: bfloat16 [8, 2, 768, 16384], P('scen', None, None, 'col'), may hold values from -0.0546875 to 0.0546875
- shared_seed: float32 [4, 4096, 256], P('col', 'scen'), may hold values from -6 to 6
- shared_inverse: float32 [8, 4, 512, 4, 4096], P(None, None, None, 'col', 'scen')
Outputs:
- private_adjoint: float32 [8, 4, 2, 768, 256], P('scen', 'col')
- shared_adjoint: float32 [4, 4096, 256], P('col')
The draws below stay inside these ranges and needn't reach their ends.
Inputs may be any that keep to these rules, and one draw needn't show every extreme that they name: `private_inverse`: each 768 x 768 block is upper triangular.
All inputs are finite; a program needn't handle non-finite values.
Results may differ from the reference program's by a relative error of at most 0.0024.
Values sent between devices are 32-bit elements; how exact they have to be, the bound alone decides.
No kernel may reach another device: no remote copies, remote signals or barrier semaphores. Data moves between devices by JAX's collectives and lax.ppermute only.
A program may use at most 192 MiB of HBM per device.

```python
import jax
import jax.numpy as jnp
from jax import lax

P_SIZE = 768
NSH = 16384
SEEDS = 256
BLK = 2
SHC = 4096
SUB = 512
N_SCEN = 8
N_COL = 4


def draw_private_inverse(key, part):
    shape = (N_SCEN, N_COL, BLK, P_SIZE, P_SIZE)
    first_key, second_key = jax.random.split(jax.random.fold_in(key, 11))
    spread = jax.random.normal(first_key, shape, jnp.float32) * (0.6 / P_SIZE ** 0.5)
    diagonal = jnp.exp(jax.random.uniform(second_key, shape[:-1], jnp.float32, -0.6931472, 0.6931472))
    row_index = lax.broadcasted_iota(jnp.int32, (P_SIZE, P_SIZE), 0)
    col_index = lax.broadcasted_iota(jnp.int32, (P_SIZE, P_SIZE), 1)
    upper = jnp.where(col_index > row_index, spread, 0.0)
    return upper + jnp.where(col_index == row_index, diagonal[..., None], 0.0)


def draw_shared_inverse(key, part):
    shape = (N_SCEN, N_COL, SUB, N_COL, SHC)
    first_key, second_key = jax.random.split(jax.random.fold_in(key, 23))
    spread = jax.random.normal(first_key, shape, jnp.float32) * (1.0 / NSH ** 0.5)
    diagonal = jax.random.uniform(second_key, shape, jnp.float32, 1.0, 2.0)
    row_global = lax.broadcasted_iota(jnp.int32, (N_SCEN, N_COL, SUB, 1, 1), 1) * SHC + lax.broadcasted_iota(jnp.int32, (N_SCEN, N_COL, SUB, 1, 1), 0) * SUB + lax.broadcasted_iota(jnp.int32, (N_SCEN, N_COL, SUB, 1, 1), 2)
    col_global = lax.broadcasted_iota(jnp.int32, (1, 1, 1, N_COL, SHC), 3) * SHC + lax.broadcasted_iota(jnp.int32, (1, 1, 1, N_COL, SHC), 4)
    return spread + jnp.where(row_global == col_global, diagonal, 0.0)


def level_of(own_key, dims, cuts, smallest, largest):
    gain, own = 1.0, jax.random.fold_in(own_key, 6)
    for dim, blocks in cuts:
        draws = jnp.exp(jax.random.uniform(jax.random.fold_in(own, dim), (blocks,), jnp.float32, smallest / len(cuts), largest / len(cuts)))
        gain = gain * jnp.repeat(draws, dims[dim] // blocks).reshape([-1 if axis == dim else 1 for axis in range(len(dims))])
    return gain


def normal_values(rng, extent, width, bound, cuts=(), held_as=jnp.bfloat16):
    entries = jax.random.normal(rng, extent, jnp.float32) * width
    if len(cuts) > 0:
        entries = level_of(rng, extent, cuts, -0.22, 0.18) * entries
    return jnp.clip(entries, min=-bound, max=bound).astype(held_as)


def setup_inputs(seed: int = 0) -> dict:
    splits = jax.random.split(jax.random.key(seed), 6)
    private_seeds = normal_values(splits[0], (N_SCEN, N_COL, BLK, P_SIZE, SEEDS), 1.0, 6.0, ((0, 8), (1, 4)), jnp.float32)
    private_inverse = draw_private_inverse(jax.random.fold_in(splits[5], 71), 0)
    coupling = normal_values(splits[2], (N_SCEN, BLK, P_SIZE, NSH), (P_SIZE * N_SCEN * BLK) ** -0.5, 0.0546875, ((0, 8), (3, 4)))
    shared_seed = normal_values(splits[3], (N_COL, SHC, SEEDS), 1.0, 6.0, ((0, 4), (1, 8)), jnp.float32)
    shared_inverse = draw_shared_inverse(jax.random.fold_in(splits[5], 71), 0)
    return dict(private_seeds=private_seeds, private_inverse=private_inverse, coupling=coupling, shared_seed=shared_seed, shared_inverse=shared_inverse)


def coupled_sum(pair):
    block_coupling, block_adjoint = pair
    return lax.dot_general(block_coupling, block_adjoint, (((0,), (0,)), ((), ())), preferred_element_type=jnp.float32)


def coupled_product(pair):
    block_coupling, shard_adjoint = pair
    return jnp.dot(block_coupling, shard_adjoint, preferred_element_type=jnp.float32)


def reference(private_seeds, private_inverse, coupling, shared_seed, shared_inverse):
    highest = lax.Precision.HIGHEST
    first = jnp.einsum("scbqp,scbqe->scbpe", private_inverse, private_seeds, precision=highest)
    first_half = first.astype(jnp.bfloat16)
    coupled = coupling.reshape(N_SCEN, BLK, P_SIZE, N_COL, SHC)
    coupled = jnp.moveaxis(coupled, 3, 0).reshape(N_COL, N_SCEN * BLK * P_SIZE, SHC)
    halves = jnp.moveaxis(first_half, 1, 0).reshape(N_COL, N_SCEN * BLK * P_SIZE, SEEDS)
    seed_sum = lax.map(coupled_sum, (coupled, halves))
    reduced = shared_seed - seed_sum
    applied = jnp.einsum("tkrcj,cje->ktre", shared_inverse, reduced, precision=highest)
    shared_adjoint = applied.reshape(N_COL, SHC, SEEDS)
    shared_half = shared_adjoint.astype(jnp.bfloat16)
    products = lax.map(coupled_product, (coupled, shared_half))
    products = jnp.moveaxis(products.reshape(N_COL, N_SCEN, BLK, P_SIZE, SEEDS), 0, 1)
    second = first - products
    private_adjoint = jnp.einsum("scbpq,scbqe->scbpe", private_inverse, second, precision=highest)
    return private_adjoint, shared_adjoint
```

```python
import functools

import jax
import jax.numpy as jnp
from jax import lax
from jax.experimental import pallas as pl
from jax.experimental.pallas import tpu as pltpu
from jax.sharding import PartitionSpec as P

F32, BF16 = jnp.float32, jnp.bfloat16
AXES = ("scen", "col")
VMEM_LIMIT = 40 * 1024 * 1024


def split(value):
    high = value.astype(BF16)
    return high, (value - high.astype(F32)).astype(BF16)


def dot(left, right):
    return jnp.dot(left, right, preferred_element_type=F32)


def dot3(left, right):
    (left_high, left_low), (right_high, right_low) = left, right
    return dot(left_high, right_high) + (dot(left_low, right_high) + dot(left_high, right_low))


def tile_of(width):
    return 256 if width % 256 == 0 else width


def call(kernel, grid, in_specs, out_specs, out_shape, flops, moved, prefetch=1, **more):
    return pl.pallas_call(
        kernel,
        grid_spec=pltpu.PrefetchScalarGridSpec(
            num_scalar_prefetch=prefetch, grid=grid, in_specs=in_specs, out_specs=out_specs
        ),
        out_shape=out_shape,
        compiler_params=pltpu.CompilerParams(vmem_limit_bytes=VMEM_LIMIT),
        cost_estimate=pl.CostEstimate(flops=int(flops), bytes_accessed=int(moved), transcendentals=0),
        **more,
    )


def unit_at(order, step, place):
    free = order[step + 1 :]
    unit = 1 << order[step] if step < len(order) else 0
    for j, bit in enumerate(free):
        unit = unit | (((place >> (len(free) - 1 - j)) & 1) << bit)
    return unit


def units_in(order, step):
    return 1 << max(len(order) - 1 - step, 0)


def first_kernel(seeds_ref, inverse_ref, first_ref, half_ref):
    width = inverse_ref.shape[1]
    tile = tile_of(width)
    seeds = split(seeds_ref[0].T)
    inverse = split(inverse_ref[0])
    for start in range(0, width, tile):
        stop = start + tile
        first = dot3(
            [part[:, :stop] for part in seeds], [part[:stop, start:stop] for part in inverse]
        )
        first_ref[:, start:stop] = first
        half_ref[:, start:stop] = first.astype(BF16)


def first_of(seeds, inverse):
    blocks, width, count = seeds.shape
    across = pl.BlockSpec((count, width), lambda b: (0, b))
    return call(
        first_kernel,
        (blocks,),
        [
            pl.BlockSpec((1, width, count), lambda b: (b, 0, 0)),
            pl.BlockSpec((1, width, width), lambda b: (b, 0, 0)),
        ],
        [across, across],
        [
            jax.ShapeDtypeStruct((count, blocks * width), F32),
            jax.ShapeDtypeStruct((count, blocks * width), BF16),
        ],
        6 * blocks * width * width * count,
        4 * blocks * width * (width + 3 * count),
        prefetch=0,
    )(seeds, inverse)


def seed_kernel(me_ref, coupling_ref, half_ref, *refs):
    *received, sum_ref = refs
    total = dot(half_ref[...], coupling_ref[...])
    for ref in received:
        total = total + ref[0]
    sum_ref[0] = total


def reduced_kernel(me_ref, coupling_ref, half_ref, seed_ref, *refs):
    *received, high_ref, low_ref = refs
    total = dot(half_ref[...], coupling_ref[...])
    for ref in received:
        total = total + ref[0]
    high_ref[...], low_ref[...] = split(seed_ref[...] - total.T)


def seed_step(me, coupling, half, seed, received, order, step, offset, cols):
    count = half.shape[0]
    depth, shard_cols = coupling.shape
    sub = seed.shape[0]
    units = units_in(order, step)
    last = step == len(order)

    def columns(f, me_ref):
        return 0, ((unit_at(order, step, f) ^ me_ref[0]) * sub + offset) // cols

    in_specs = [
        pl.BlockSpec((depth, cols), columns),
        pl.BlockSpec((count, depth), lambda f, me_ref: (0, 0)),
    ]
    operands = [coupling, half]
    if last:
        in_specs.append(pl.BlockSpec((cols, count), lambda f, me_ref: (offset // cols, 0)))
        operands.append(seed)
        place = pl.BlockSpec((cols, count), lambda f, me_ref: (0, 0))
        out_specs = [place, place]
        out_shape = [jax.ShapeDtypeStruct((cols, count), BF16)] * 2
    else:
        out_specs = pl.BlockSpec((1, count, cols), lambda f, me_ref: (f, 0, 0))
        out_shape = jax.ShapeDtypeStruct((units, count, cols), F32)
    first_place = 0 if last else units
    for array in received:
        in_specs.append(
            pl.BlockSpec((1, count, cols), lambda f, me_ref: (first_place + f, 0, 0))
        )
        operands.append(array)
    return call(
        reduced_kernel if last else seed_kernel,
        (units,),
        in_specs,
        out_specs,
        out_shape,
        2 * units * depth * cols * count,
        units * cols * (2 * depth + 4 * count * (1 + len(received))),
    )(me, *operands)


def shared_kernel(group, rows, parts, me_ref, *refs):
    tiles, refs = refs[:group], refs[group:]
    highs, refs = refs[:parts], refs[parts:]
    lows, refs = refs[:parts], refs[parts:]
    *received, out_ref = refs
    depth = highs[0].shape[0]
    lanes = tiles[0].shape[2]
    pieces = depth // lanes
    stride = pieces * parts
    for g in range(group):
        total = None
        for part in range(parts):
            tile = [
                tiles[g][0, pl.ds(part * pieces + piece, rows, stride=stride), :]
                if stride > 1
                else tiles[g][0]
                for piece in range(pieces)
            ]
            tile = tile[0] if pieces == 1 else jnp.concatenate(tile, axis=1)
            term = dot3(split(tile), (highs[part][...], lows[part][...]))
            total = term if total is None else total + term
        for ref in received:
            total = total + ref[g]
        out_ref[g] = total


def shared_step(me, tiles, highs, lows, received, order, step, offset, rows):
    depth, count = highs[0].shape
    lanes = tiles.shape[2]
    parts = len(highs)
    stride = parts * depth // lanes
    units = units_in(order, step)
    group = min(units, 4)
    first_place = 0 if step == len(order) else units // group

    def tile_place(g, f, me_ref):
        return unit_at(order, step, f * group + g) ^ me_ref[0], offset // rows, 0

    whole = pl.BlockSpec((depth, count), lambda f, me_ref: (0, 0))
    in_specs = [
        pl.BlockSpec((1, rows * stride, lanes), functools.partial(tile_place, g))
        for g in range(group)
    ]
    in_specs += [whole] * (2 * parts)
    in_specs += [
        pl.BlockSpec((group, rows, count), lambda f, me_ref: (first_place + f, 0, 0))
    ] * len(received)
    return call(
        functools.partial(shared_kernel, group, rows, parts),
        (units // group,),
        in_specs,
        pl.BlockSpec((group, rows, count), lambda f, me_ref: (f, 0, 0)),
        jax.ShapeDtypeStruct((units, rows, count), F32),
        6 * units * rows * parts * depth * count,
        4 * units * rows * (parts * depth + count * (1 + len(received))),
    )(me, *([tiles] * group), *highs, *lows, *received)


def coupled_kernel(groups, chunks, aliased, me_ref, coupling_ref, start_ref, *refs):
    pieces = refs[: groups * chunks]
    second_ref, adjoint_ref = refs[-2:]
    u = pl.program_id(0)

    @pl.when(u == 0)
    def _():
        second_ref[...] = start_ref[...]

    for g in range(groups):

        @pl.when(u == g)
        def _():
            rows = [ref[0] for ref in pieces[g * chunks : (g + 1) * chunks]]
            block = jnp.concatenate(rows, axis=0)
            adjoint_ref[...] = block
            second_ref[...] -= dot(coupling_ref[...], block.astype(BF16))


def coupled_step(me, coupling, start, pieces, units, adjoint):
    depth, count = start.shape
    chunks = len(pieces[0])
    sub = sum(piece.shape[1] for piece in pieces[0])
    groups = len(units)

    def unit_of(u):
        unit = units[-1]
        for g in range(groups - 1):
            unit = jnp.where(u == g, units[g], unit)
        return unit

    in_specs = [
        pl.BlockSpec((depth, sub), lambda u, me_ref: (0, unit_of(u) ^ me_ref[0])),
        pl.BlockSpec((depth, count), lambda u, me_ref: (0, 0)),
    ]
    operands = [coupling, start]
    for group in pieces:
        for piece in group:
            in_specs.append(pl.BlockSpec(piece.shape, lambda u, me_ref: (0, 0, 0)))
            operands.append(piece)
    more = {}
    if adjoint is not None:
        in_specs.append(pl.BlockSpec(memory_space=pl.ANY))
        operands.append(adjoint)
        more["input_output_aliases"] = {len(operands): 1}
    return call(
        functools.partial(coupled_kernel, groups, chunks, adjoint is not None),
        (groups,),
        in_specs,
        [
            pl.BlockSpec((depth, count), lambda u, me_ref: (0, 0)),
            pl.BlockSpec((sub, count), lambda u, me_ref: (unit_of(u) ^ me_ref[0], 0)),
        ],
        [
            jax.ShapeDtypeStruct((depth, count), F32),
            jax.ShapeDtypeStruct((coupling.shape[1], count), F32),
        ],
        2 * groups * depth * sub * count,
        groups * sub * (2 * depth + 8 * count) + 8 * depth * count,
        **more,
    )(me, *operands)


def private_kernel(inverse_ref, second_ref, out_ref):
    width = inverse_ref.shape[1]
    tile = tile_of(width)
    inverse = split(inverse_ref[0])
    second = split(second_ref[0])
    for start in range(0, width, tile):
        out_ref[0, start : start + tile] = dot3(
            [part[start : start + tile, start:] for part in inverse],
            [part[start:] for part in second],
        )


def private_of(inverse, second):
    blocks, width, count = second.shape
    return call(
        private_kernel,
        (blocks,),
        [
            pl.BlockSpec((1, width, width), lambda b: (b, 0, 0)),
            pl.BlockSpec((1, width, count), lambda b: (b, 0, 0)),
        ],
        pl.BlockSpec((1, width, count), lambda b: (b, 0, 0)),
        jax.ShapeDtypeStruct((blocks, width, count), F32),
        6 * blocks * width * width * count,
        4 * blocks * width * (width + 2 * count),
        prefetch=0,
    )(inverse, second)


def on_device(scen_count, col_count, private_seeds, private_inverse, coupling, shared_seed, shared_inverse):
    blocks, width = private_inverse.shape[2:4]
    count = private_seeds.shape[4]
    shard_cols = coupling.shape[3]
    sub = shared_seed.shape[1]
    depth = shared_inverse.shape[4]
    devices = scen_count * col_count
    scen_bits, col_bits = scen_count.bit_length() - 1, col_count.bit_length() - 1

    my_scen, my_col = lax.axis_index("scen"), lax.axis_index("col")
    me_scen = my_scen.astype(jnp.int32).reshape(1)
    me = (my_scen * col_count + my_col).astype(jnp.int32).reshape(1)

    def exchange(array, bit):
        return lax.ppermute(array, AXES, [(w, w ^ (1 << bit)) for w in range(devices)])

    flat_coupling = coupling[0].reshape(blocks * width, shard_cols)
    first, half = first_of(private_seeds[0, 0], private_inverse[0, 0])
    first = first.T

    rest = list(range(1, scen_bits))
    seed_orders = [[0] + rest, [0] + rest[::-1]]
    cols = sub // 2 if sub % 256 == 0 else sub
    highs, lows = [], []
    received = [[] for _ in range(sub // cols)]
    for step in range(scen_bits + 1):
        for chunk in range(sub // cols):
            order = seed_orders[chunk]
            out = seed_step(
                me_scen, flat_coupling, half, shared_seed[0], received[chunk], order, step,
                chunk * cols, cols,
            )
            if step < scen_bits:
                received[chunk].append(exchange(out, order[step] + col_bits))
            else:
                highs.append(out[0])
                lows.append(out[1])

    lanes = min(depth, 128)
    tiles = shared_inverse.reshape(devices, sub * depth // lanes, lanes)
    col_order = list(range(col_bits))
    core = col_bits
    outer = [bit + col_bits for bit in rest]
    unit = sub // 8
    chunks = [
        (0, 3 * unit, [core] + outer + col_order, outer),
        (3 * unit, 3 * unit, [core] + outer[::-1] + col_order, outer[::-1]),
        (6 * unit, 2 * unit, [core] + col_order + outer, outer),
    ]
    received = [[] for _ in chunks]
    mine = []
    steps = scen_bits + col_bits
    for step in range(steps + 1):
        for index, (offset, rows, order, _) in enumerate(chunks):
            out = shared_step(
                me, tiles, highs, lows, received[index], order, step, offset, rows
            )
            if step < steps:
                received[index].append(exchange(out, order[step]))
            else:
                mine.append(out)

    near = [{0: piece} for piece in mine]
    for index, (_, _, _, spread) in enumerate(chunks):
        for bit in spread:
            for unit_number, piece in list(near[index].items()):
                near[index][unit_number | (1 << (bit - col_bits))] = exchange(piece, bit)
    far = [
        {unit_number | 1: exchange(piece, core) for unit_number, piece in held.items()}
        for held in near
    ]

    second, adjoint = first, None
    for held in (near, far):
        units = sorted(held[0])
        second, adjoint = coupled_step(
            me_scen, flat_coupling, second, [[part[u] for part in held] for u in units], units, adjoint
        )
    private_adjoint = private_of(private_inverse[0, 0], second.reshape(blocks, width, count))
    return private_adjoint[None, None], adjoint[None]


def solution(mesh):
    in_specs = (
        P("scen", "col", None, None, None),
        P("scen", "col", None, None, None),
        P("scen", None, None, "col"),
        P("col", "scen", None),
        P(None, None, None, "col", "scen"),
    )
    out_specs = (P("scen", "col", None, None, None), P("col", None, None))
    return jax.shard_map(
        functools.partial(on_device, mesh.shape["scen"], mesh.shape["col"]),
        mesh=mesh,
        in_specs=in_specs,
        out_specs=out_specs,
        check_vma=False,
    )
```

```python
import functools
import math

import jax
import jax.numpy as jnp
from jax import lax
from jax.experimental import pallas as pl
from jax.experimental.pallas import tpu as pltpu
from jax.sharding import PartitionSpec as P

F32, BF16 = jnp.float32, jnp.bfloat16
AXES = ("scen", "col")
MIB = 1024 * 1024


def split(value):
    high = value.astype(BF16)
    return high, (value - high.astype(F32)).astype(BF16)


def dot(left, right):
    return jnp.dot(left, right, preferred_element_type=F32)


def dot3(left, right):
    (left_high, left_low), (right_high, right_low) = left, right
    return dot(left_high, right_high) + (dot(left_low, right_high) + dot(left_high, right_low))


def tile_of(width):
    return 256 if width % 256 == 0 else width


def bytes_of(spec, dtype):
    shape = spec.block_shape
    return 0 if shape is None else math.prod(shape) * dtype.itemsize


def call(kernel, grid, in_specs, out_specs, out_shape, flops, moved, prefetch=1, scratch=(), room=None, earlier=(), **more):
    inputs = prefetch + len(in_specs)
    body = kernel
    if earlier:
        body = lambda *refs: kernel(*refs[:inputs], *refs[inputs + len(earlier) :])
    in_specs = list(in_specs) + [pl.BlockSpec(memory_space=pl.ANY)] * len(earlier)

    def run(*operands):
        operands += tuple(earlier)
        outs = out_shape if isinstance(out_shape, (list, tuple)) else [out_shape]
        specs = out_specs if isinstance(out_specs, (list, tuple)) else [out_specs]
        need = sum(2 * bytes_of(s, o.dtype) for s, o in zip(in_specs, operands[prefetch:]))
        need += sum(2 * bytes_of(s, o.dtype) for s, o in zip(specs, outs))
        need += sum(
            math.prod(s.shape) * jnp.dtype(s.dtype).itemsize for s in scratch if len(s.shape) > 1
        )
        return pl.pallas_call(
            body,
            grid_spec=pltpu.PrefetchScalarGridSpec(
                num_scalar_prefetch=prefetch,
                grid=grid,
                in_specs=in_specs,
                out_specs=out_specs,
                scratch_shapes=list(scratch),
            ),
            out_shape=out_shape,
            compiler_params=pltpu.CompilerParams(vmem_limit_bytes=room or need + 10 * MIB),
            cost_estimate=pl.CostEstimate(
                flops=int(flops), bytes_accessed=int(moved), transcendentals=0
            ),
            **more,
        )(*operands)

    return run


def spread(bits, place):
    unit = 0
    for j, bit in enumerate(bits):
        unit = unit | (((place >> (len(bits) - 1 - j)) & 1) << bit)
    return unit


def unit_at(order, step, place):
    return (1 << order[step] if step < len(order) else 0) | spread(order[step + 1 :], place)


def units_in(order, step):
    return 1 << max(len(order) - 1 - step, 0)


def first_kernel(seeds_ref, inverse_ref, first_ref, half_ref):
    width = inverse_ref.shape[1]
    tile = tile_of(width)
    seeds = split(seeds_ref[0].T)
    inverse = split(inverse_ref[0])
    for start in range(0, width, tile):
        stop = start + tile
        first = dot3(
            [part[:, :stop] for part in seeds], [part[:stop, start:stop] for part in inverse]
        )
        first_ref[:, start:stop] = first
        half_ref[:, start:stop] = first.astype(BF16)


def first_of(seeds, inverse):
    blocks, width, count = seeds.shape
    across = pl.BlockSpec((count, width), lambda b: (0, b))
    return call(
        first_kernel,
        (blocks,),
        [
            pl.BlockSpec((1, width, count), lambda b: (b, 0, 0)),
            pl.BlockSpec((1, width, width), lambda b: (b, 0, 0)),
        ],
        [across, across],
        [
            jax.ShapeDtypeStruct((count, blocks * width), F32),
            jax.ShapeDtypeStruct((count, blocks * width), BF16),
        ],
        6 * blocks * width * width * count,
        4 * blocks * width * (width + 3 * count),
        prefetch=0,
        room=58 * MIB,
    )(seeds, inverse)


def seed_kernel(me_ref, coupling_ref, half_ref, sum_ref):
    sum_ref[0] = dot(half_ref[...], coupling_ref[...])


def seed_products(me, coupling, half, sub, bits, base, offset, cols, earlier=()):
    count, depth = half.shape
    units = 1 << len(bits)

    def columns(f, me_ref):
        return 0, (((spread(bits, f) | base) ^ me_ref[0]) * sub + offset) // cols

    return call(
        seed_kernel,
        (units,),
        [
            pl.BlockSpec((depth, cols), columns),
            pl.BlockSpec((count, depth), lambda f, me_ref: (0, 0)),
        ],
        pl.BlockSpec((1, count, cols), lambda f, me_ref: (f, 0, 0)),
        jax.ShapeDtypeStruct((units, count, cols), F32),
        2 * units * depth * cols * count,
        units * cols * (2 * depth + 4 * count),
        room=52 * MIB,
        earlier=earlier,
    )(me, coupling, half)


def sum_kernel(terms, *refs):
    out_ref = refs[terms]
    out_ref[0] = sum(ref[0] for ref in refs[:terms])


def sum_of(terms, count, cols, chosen, free, earlier):
    def place(bits, block, g):
        unit = spread(free, g) | chosen
        at = 0
        for bit in bits:
            at = at * 2 + ((unit >> bit) & 1)
        return at, 0, block

    units = 1 << len(free)
    return call(
        functools.partial(sum_kernel, len(terms)),
        (units,),
        [
            pl.BlockSpec((1, count, cols), functools.partial(place, bits, block))
            for _, bits, block in terms
        ],
        pl.BlockSpec((1, count, cols), lambda g: (g, 0, 0)),
        jax.ShapeDtypeStruct((units, count, cols), F32),
        0,
        4 * units * count * cols * (1 + len(terms)),
        prefetch=0,
        earlier=earlier,
    )(*[array for array, _, _ in terms])


def reduced_kernel(cols, chunks, seed_ref, *refs):
    *terms, out_ref = refs
    each = len(terms) // chunks
    for chunk in range(chunks):
        place = pl.ds(chunk * cols, cols)
        total = sum(ref[0] for ref in terms[chunk * each : (chunk + 1) * each])
        out_ref[place] = seed_ref[place] - total.T


def reduced_of(seed, terms, cols):
    count = seed.shape[1]
    whole = pl.BlockSpec(seed.shape, lambda i: (0, 0))
    flat = [term for chunk in terms for term in chunk]
    return call(
        functools.partial(reduced_kernel, cols, len(terms)),
        (1,),
        [whole]
        + [
            pl.BlockSpec((1, count, cols), functools.partial(lambda block, i: (0, 0, block), block))
            for _, block in flat
        ],
        whole,
        jax.ShapeDtypeStruct(seed.shape, F32),
        0,
        16 * seed.size,
        prefetch=0,
    )(seed, *[array for array, _ in flat])


def rows_of(tile_ref, rows, pieces):
    if pieces == 1:
        return tile_ref[0]
    return jnp.concatenate(
        [tile_ref[0, pl.ds(piece, rows, stride=pieces), :] for piece in range(pieces)], axis=1
    )


def packed_kernel(group, rows, pieces, me_ref, *refs):
    out_ref = refs[-1]
    for g in range(group):
        out_ref[g] = rows_of(refs[g], rows, pieces)


def packed_for_pair(me, tiles, bits, base, offset, rows, pieces, earlier):
    lanes = tiles.shape[2]
    units = 1 << len(bits)
    group = min(units, 4)

    def place(g, f, me_ref):
        return (spread(bits, f * group + g) | base) ^ me_ref[0], offset // rows, 0

    return call(
        functools.partial(packed_kernel, group, rows, pieces),
        (units // group,),
        [
            pl.BlockSpec((1, rows * pieces, lanes), functools.partial(place, g))
            for g in range(group)
        ],
        pl.BlockSpec((group, rows, pieces * lanes), lambda f, me_ref: (f, 0, 0)),
        jax.ShapeDtypeStruct((units, rows, pieces * lanes), F32),
        0,
        8 * units * rows * pieces * lanes,
        room=34 * MIB,
        earlier=earlier,
    )(me, *([tiles] * group))


def shared_kernel(group, rows, pieces, paired, me_ref, *refs):
    tiles, refs = refs[:group], refs[group:]
    others, refs = (refs[:group], refs[group:]) if paired else ((), refs)
    seeds, refs = refs[: 1 + paired], refs[1 + paired :]
    *received, out_ref, high_ref, low_ref, seed_high_ref, seed_low_ref = refs
    depth = seeds[0].shape[0]

    @pl.when(pl.program_id(0) == 0)
    def _():
        for side, ref in enumerate(seeds):
            place = pl.ds(side * depth, depth)
            seed_high_ref[place], seed_low_ref[place] = split(ref[...])

    for g in range(group):
        place = pl.ds(g * rows, rows)
        high_ref[place, :depth], low_ref[place, :depth] = split(rows_of(tiles[g], rows, pieces))
        if paired:
            high_ref[place, depth:], low_ref[place, depth:] = split(others[g][0])
    total = dot3((high_ref[...], low_ref[...]), (seed_high_ref[...], seed_low_ref[...]))
    for g in range(group):
        term = total[g * rows : (g + 1) * rows]
        for ref in received:
            term = term + ref[g]
        out_ref[g] = term


def shared_step(me, tiles, others, seeds, received, order, step, offset, rows, core):
    depth, count = seeds[0].shape
    lanes = tiles.shape[2]
    pieces = depth // lanes
    units = units_in(order, step)
    group = min(4, max(units // 2, 1))
    first_place = 0 if step == len(order) else units // group
    paired = others is not None

    def tile_place(g, f, me_ref):
        return unit_at(order, step, f * group + g) ^ me_ref[0], offset // rows, 0

    def other_place(g, f, me_ref):
        unit = unit_at(order, step, f * group + g)
        return (unit >> (core + 1) << core) | (unit & ((1 << core) - 1)), 0, 0

    whole = pl.BlockSpec((depth, count), lambda f, me_ref: (0, 0))
    in_specs = [
        pl.BlockSpec((1, rows * pieces, lanes), functools.partial(tile_place, g))
        for g in range(group)
    ]
    operands = [tiles] * group
    if paired:
        in_specs += [
            pl.BlockSpec((1, rows, depth), functools.partial(other_place, g)) for g in range(group)
        ]
        operands += [others] * group
    else:
        seeds = seeds[:1]
    in_specs += [whole] * len(seeds)
    in_specs += [
        pl.BlockSpec((group, rows, count), lambda f, me_ref: (first_place + f, 0, 0))
    ] * len(received)
    reach = depth * len(seeds)
    halves = pltpu.VMEM((group * rows, reach), BF16)
    seed_halves = pltpu.VMEM((reach, count), BF16)
    return call(
        functools.partial(shared_kernel, group, rows, pieces, paired),
        (units // group,),
        in_specs,
        pl.BlockSpec((group, rows, count), lambda f, me_ref: (f, 0, 0)),
        jax.ShapeDtypeStruct((units, rows, count), F32),
        6 * units * rows * reach * count,
        4 * units * rows * (reach + count * (1 + len(received))),
        scratch=[halves, halves, seed_halves, seed_halves],
        room=34 * MIB,
    )(me, *operands, *seeds, *received)


def coupled_kernel(groups, chunks, aliased, last, me_ref, coupling_ref, start_ref, *refs):
    pieces, refs = refs[: groups * chunks], refs[groups * chunks :]
    if aliased:
        refs = refs[1:]
    u = pl.program_id(0)
    if last:
        inverse_ref, out_ref, adjoint_ref, second_ref, held_ref, sem = refs
        fetch = pltpu.make_async_copy(inverse_ref, held_ref, sem)
    else:
        second_ref, adjoint_ref = refs

    @pl.when(u == 0)
    def _():
        if last:
            fetch.start()
        second_ref[...] = start_ref[...]

    for g in range(groups):

        @pl.when(u == g)
        def _():
            rows = [ref[0] for ref in pieces[g * chunks : (g + 1) * chunks]]
            block = jnp.concatenate(rows, axis=0)
            adjoint_ref[...] = block
            second_ref[...] -= dot(coupling_ref[...], block.astype(BF16))

    if last:

        @pl.when(u == groups - 1)
        def _():
            fetch.wait()
            blocks, width, _ = held_ref.shape
            tile = tile_of(width)
            for block in range(blocks):
                second = split(second_ref[block * width : (block + 1) * width])
                for start in range(0, width, tile):
                    out_ref[block, start : start + tile] = dot3(
                        split(held_ref[block, start : start + tile, start:]),
                        [part[start:] for part in second],
                    )


def coupled_step(me, coupling, start, pieces, units, adjoint, inverse=None):
    depth, count = start.shape
    chunks = len(pieces[0])
    sub = sum(piece.shape[1] for piece in pieces[0])
    groups = len(units)

    def unit_of(u):
        unit = units[-1]
        for g in range(groups - 1):
            unit = jnp.where(u == g, units[g], unit)
        return unit

    whole = pl.BlockSpec((depth, count), lambda u, me_ref: (0, 0))
    in_specs = [
        pl.BlockSpec((depth, sub), lambda u, me_ref: (0, unit_of(u) ^ me_ref[0])),
        whole,
    ]
    operands = [coupling, start]
    for group in pieces:
        for piece in group:
            in_specs.append(pl.BlockSpec(piece.shape, lambda u, me_ref: (0, 0, 0)))
            operands.append(piece)
    more = {}
    if adjoint is not None:
        in_specs.append(pl.BlockSpec(memory_space=pl.ANY))
        operands.append(adjoint)
        more["input_output_aliases"] = {len(operands): 1}
    flops = 2 * groups * depth * sub * count
    moved = groups * sub * (2 * depth + 8 * count) + 8 * depth * count
    out_spec, out_shape, scratch = whole, jax.ShapeDtypeStruct((depth, count), F32), ()
    if inverse is not None:
        blocks, width, _ = inverse.shape
        in_specs.append(pl.BlockSpec(memory_space=pl.ANY))
        operands.append(inverse)
        out_spec = pl.BlockSpec((blocks, width, count), lambda u, me_ref: (0, 0, 0))
        out_shape = jax.ShapeDtypeStruct((blocks, width, count), F32)
        scratch = (
            pltpu.VMEM((depth, count), F32),
            pltpu.VMEM(inverse.shape, F32),
            pltpu.SemaphoreType.DMA(()),
        )
        flops += 6 * inverse.size * count
        moved += 4 * inverse.size
    return call(
        functools.partial(
            coupled_kernel, groups, chunks, adjoint is not None, inverse is not None
        ),
        (groups,),
        in_specs,
        [out_spec, pl.BlockSpec((sub, count), lambda u, me_ref: (unit_of(u) ^ me_ref[0], 0))],
        [out_shape, jax.ShapeDtypeStruct((coupling.shape[1], count), F32)],
        flops,
        moved,
        scratch=scratch,
        **more,
    )(me, *operands)


def on_device(scen_count, col_count, private_seeds, private_inverse, coupling, shared_seed, shared_inverse):
    blocks, width = private_inverse.shape[2:4]
    count = private_seeds.shape[4]
    shard_cols = coupling.shape[3]
    sub = shared_seed.shape[1]
    depth = shared_inverse.shape[4]
    devices = scen_count * col_count
    scen_bits, col_bits = scen_count.bit_length() - 1, col_count.bit_length() - 1

    my_scen, my_col = lax.axis_index("scen"), lax.axis_index("col")
    me_scen = my_scen.astype(jnp.int32).reshape(1)
    me = (my_scen * col_count + my_col).astype(jnp.int32).reshape(1)

    def exchange(array, bit):
        return lax.ppermute(array, AXES, [(w, w ^ (1 << bit)) for w in range(devices)])

    flat_coupling = coupling[0].reshape(blocks * width, shard_cols)
    first, half = first_of(private_seeds[0, 0], private_inverse[0, 0])

    core = col_bits
    col_order = list(range(col_bits))
    outer = list(range(core + 1, core + scen_bits))
    both = outer[::-1] + col_order[::-1]
    unit = sub // 8
    chunks = [
        (0, 3 * unit, True, col_order[:1] + outer + col_order[1:], outer),
        (3 * unit, 3 * unit, True, outer + col_order, outer),
        (
            6 * unit,
            2 * unit,
            False,
            [core] + outer[1:] + col_order + outer[:1],
            outer[::-1],
        ),
    ]
    lanes = min(depth, 128)
    pieces = depth // lanes
    tiles = shared_inverse.reshape(devices, sub * pieces, lanes)

    bits = list(range(scen_bits - 1, 0, -1))
    cols = sub // 2 if sub % 256 == 0 else sub
    seed_orders = [bits[::-1], bits][: sub // cols]
    from_pair, begun = [], []
    for chunk in range(len(seed_orders)):
        away = seed_products(me_scen, flat_coupling, half, sub, bits, 1, chunk * cols, cols, begun)
        from_pair.append(exchange(away, core))
        begun.append(away)
    def packed(index, earlier):
        offset, rows = chunks[index][:2]
        return packed_for_pair(me, tiles, both, 1 << core, offset, rows, pieces, earlier)

    packs = [packed(0, begun)]
    mine = seed_products(me_scen, flat_coupling, half, sub, bits, 0, 0, sub, packs)
    terms = [
        [(mine, bits, chunk), (from_pair[chunk], bits, 0)] for chunk in range(len(seed_orders))
    ]
    for step in range(len(bits)):
        begun = []
        for chunk, order in enumerate(seed_orders):
            free = [bit for bit in bits if bit not in order[: step + 1]]
            away = sum_of(
                terms[chunk], count, cols, 1 << order[step], free, packs[1:] if step == 1 else ()
            )
            begun.append(away)
            terms[chunk].append((exchange(away, order[step] + col_bits), free, 0))
        if step == 0:
            packs.append(packed(1, begun))
    others = [exchange(array, core) for array in packs] + [None]
    terms = [[(array, block) for array, _, block in chunk] for chunk in terms]
    reduced = reduced_of(shared_seed[0], terms, cols)
    seeds = [reduced, exchange(reduced, core)]

    received = [[] for _ in chunks]
    ends = [None] * len(chunks)
    for step in range(-1, len(both) + 1):
        for index, (offset, rows, paired, order, _) in enumerate(chunks):
            at = step if paired else step + 1
            if at < 0:
                continue
            out = shared_step(
                me, tiles, others[index], seeds, received[index], order, at, offset, rows, core
            )
            if at < len(order):
                received[index].append(exchange(out, order[at]))
            else:
                ends[index] = out

    near = [{0: piece} for piece in ends]
    for index, (_, _, _, _, way) in enumerate(chunks):
        for bit in way:
            for number, piece in list(near[index].items()):
                near[index][number | (1 << (bit - col_bits))] = exchange(piece, bit)
    held = [
        {**kept, **{number | 1: exchange(piece, core) for number, piece in kept.items()}}
        for kept in near
    ]

    second, adjoint = first.T, None
    everything = sorted(near[0])
    groups = [everything[:1], everything[1:-1], everything[-1:]]
    inverse = private_inverse[0, 0]
    for place, group in enumerate(groups):
        for side in ([0, 1],) if place != 1 else ([0], [1]):
            numbers = [number | core_bit for core_bit in side for number in group]
            second, adjoint = coupled_step(
                me_scen,
                flat_coupling,
                second,
                [[part[number] for part in held] for number in numbers],
                numbers,
                adjoint,
                inverse if place == len(groups) - 1 else None,
            )
    return second[None, None], adjoint[None]


def solution(mesh):
    in_specs = (
        P("scen", "col", None, None, None),
        P("scen", "col", None, None, None),
        P("scen", None, None, "col"),
        P("col", "scen", None),
        P(None, None, None, "col", "scen"),
    )
    out_specs = (P("scen", "col", None, None, None), P("col", None, None))
    return jax.shard_map(
        functools.partial(on_device, mesh.shape["scen"], mesh.shape["col"]),
        mesh=mesh,
        in_specs=in_specs,
        out_specs=out_specs,
        check_vma=False,
    )
```

```python
import functools
import math

import jax
import jax.numpy as jnp
from jax import lax
from jax.experimental import pallas as pl
from jax.experimental.pallas import tpu as pltpu
from jax.sharding import PartitionSpec as P

F32, BF16 = jnp.float32, jnp.bfloat16
AXES = ("scen", "col")
MIB = 1024 * 1024


def split(value):
    high = value.astype(BF16)
    return high, (value - high.astype(F32)).astype(BF16)


def dot(left, right):
    return jnp.dot(left, right, preferred_element_type=F32)


def dot3(left, right):
    (left_high, left_low), (right_high, right_low) = left, right
    return dot(left_high, right_high) + (dot(left_low, right_high) + dot(left_high, right_low))


def tile_of(width):
    return 256 if width % 256 == 0 else width


def bytes_of(spec, dtype):
    shape = spec.block_shape
    return 0 if shape is None else math.prod(shape) * dtype.itemsize


def call(kernel, grid, in_specs, out_specs, out_shape, flops, moved, prefetch=1, scratch=(), room=None, earlier=(), **more):
    inputs = prefetch + len(in_specs)
    body = kernel
    if earlier:
        body = lambda *refs: kernel(*refs[:inputs], *refs[inputs + len(earlier) :])
    in_specs = list(in_specs) + [pl.BlockSpec(memory_space=pl.ANY)] * len(earlier)

    def run(*operands):
        operands += tuple(earlier)
        outs = out_shape if isinstance(out_shape, (list, tuple)) else [out_shape]
        specs = out_specs if isinstance(out_specs, (list, tuple)) else [out_specs]
        need = sum(2 * bytes_of(s, o.dtype) for s, o in zip(in_specs, operands[prefetch:]))
        need += sum(2 * bytes_of(s, o.dtype) for s, o in zip(specs, outs))
        need += sum(
            math.prod(s.shape) * jnp.dtype(s.dtype).itemsize for s in scratch if len(s.shape) > 1
        )
        return pl.pallas_call(
            body,
            grid_spec=pltpu.PrefetchScalarGridSpec(
                num_scalar_prefetch=prefetch,
                grid=grid,
                in_specs=in_specs,
                out_specs=out_specs,
                scratch_shapes=list(scratch),
            ),
            out_shape=out_shape,
            compiler_params=pltpu.CompilerParams(vmem_limit_bytes=room or need + 10 * MIB),
            cost_estimate=pl.CostEstimate(
                flops=int(flops) // 1, bytes_accessed=int(moved) // 1, transcendentals=0
            ),
            **more,
        )(*operands)

    return run


def spread(bits, place):
    unit = 0
    for j, bit in enumerate(bits):
        unit = unit | (((place >> (len(bits) - 1 - j)) & 1) << bit)
    return unit


def place_of(bits, unit):
    place = 0
    for bit in bits:
        place = place * 2 + ((unit >> bit) & 1)
    return place


def first_kernel(seeds_ref, inverse_ref, first_ref, half_ref):
    width = inverse_ref.shape[1]
    tile = tile_of(width)
    seeds = split(seeds_ref[0].T)
    inverse = split(inverse_ref[0])
    for start in range(0, width, tile):
        stop = start + tile
        first = dot3(
            [part[:, :stop] for part in seeds], [part[:stop, start:stop] for part in inverse]
        )
        first_ref[:, start:stop] = first
        half_ref[:, start:stop] = first.astype(BF16)


def first_of(seeds, inverse):
    blocks, width, count = seeds.shape
    across = pl.BlockSpec((count, width), lambda b: (0, b))
    return call(
        first_kernel,
        (blocks,),
        [
            pl.BlockSpec((1, width, count), lambda b: (b, 0, 0)),
            pl.BlockSpec((1, width, width), lambda b: (b, 0, 0)),
        ],
        [across, across],
        [
            jax.ShapeDtypeStruct((count, blocks * width), F32),
            jax.ShapeDtypeStruct((count, blocks * width), BF16),
        ],
        6 * blocks * width * width * count,
        4 * blocks * width * (width + 3 * count),
        prefetch=0,
    )(seeds, inverse)


def seed_kernel(me_ref, coupling_ref, half_ref, *sum_refs):
    total = dot(half_ref[...], coupling_ref[...])
    cols = total.shape[1] // len(sum_refs)
    for chunk, ref in enumerate(sum_refs):
        ref[0] = total[:, chunk * cols : (chunk + 1) * cols]


def seed_products(me, coupling, half, sub, orders, base, offset):
    count, depth = half.shape
    cols = seed_cols(sub)
    wide = cols * len(orders)
    units = 1 << len(orders[0])

    def unit_of(f):
        return spread(orders[0], f) | base

    return call(
        seed_kernel,
        (units,),
        [
            pl.BlockSpec(
                (depth, wide), lambda f, me_ref: (0, ((unit_of(f) ^ me_ref[0]) * sub + offset) // wide)
            ),
            pl.BlockSpec((count, depth), lambda f, me_ref: (0, 0)),
        ],
        [
            pl.BlockSpec(
                (1, count, cols),
                functools.partial(
                    lambda order, f, me_ref: (place_of(order, unit_of(f)), 0, 0), order
                ),
            )
            for order in orders
        ],
        [jax.ShapeDtypeStruct((units, count, cols), F32)] * len(orders),
        2 * units * depth * wide * count,
        units * wide * (2 * depth + 4 * count),
    )(me, coupling, half)


def seed_cols(sub):
    return sub // 2 if sub % 256 == 0 else sub


def reduced_kernel(chunks, seed_ref, *refs):
    *terms, out_ref = refs
    each = len(terms) // chunks
    cols = terms[0].shape[2]
    for chunk in range(chunks):
        place = pl.ds(chunk * cols, cols)
        total = sum(ref[0] for ref in terms[chunk * each : (chunk + 1) * each])
        out_ref[place] = seed_ref[place] - total.T


def reduced_of(seed, terms):
    whole = pl.BlockSpec(seed.shape, lambda i: (0, 0))
    flat = [term for chunk in terms for term in chunk]
    return call(
        functools.partial(reduced_kernel, len(terms)),
        (1,),
        [whole] + [pl.BlockSpec((1, *term.shape[1:]), lambda i: (0, 0, 0)) for term in flat],
        whole,
        jax.ShapeDtypeStruct(seed.shape, F32),
        0,
        16 * seed.size,
        prefetch=0,
    )(seed, *flat)


def rows_of(tile_ref, rows, pieces):
    if pieces == 1:
        return tile_ref[0]
    lanes = tile_ref.shape[2]
    parts = tile_ref[0].reshape(rows // 8, pieces, 8, lanes)
    parts = [parts[:, j] for j in range(pieces)]
    at = lax.broadcasted_iota(jnp.int32, (rows // 8, 8, lanes), 1)
    step = 1
    while step < pieces:
        upper = (at & step) != 0
        for j in range(pieces):
            if j & step == 0:
                low, high = parts[j], parts[j + step]
                parts[j] = jnp.where(upper, pltpu.roll(high, step, 1), low)
                parts[j + step] = jnp.where(upper, high, pltpu.roll(low, 8 - step, 1))
        step *= 2
    return jnp.concatenate([part.reshape(rows, lanes) for part in parts], axis=1)


def share_kernel(chunks, pieces, *refs):
    terms, out_ref, held_ref, order_ref = refs[:-3], *refs[-3:]
    each = len(terms) // chunks
    rows = terms[0].shape[1]
    run = 8 // pieces
    total = jnp.concatenate(
        [sum(ref[0] for ref in terms[at : at + each]) for at in range(0, len(terms), each)], axis=0
    )
    for lane in range(0, total.shape[1], 128):
        held_ref[...] = total[:, lane : lane + 128]
        for place in range(8):
            j, b = place // run, place % run
            order_ref[pl.ds(place, chunks * rows // 8, stride=8), :] = held_ref[
                pl.ds(b * pieces + j, chunks * rows // 8, stride=8), :
            ]
        out_ref[:, lane : lane + 128] = order_ref[...]


def share_of(terms, pieces):
    _, rows, count = terms[0][0].shape
    flat = [term for chunk in terms for term in chunk]
    shape = (len(terms) * rows, count)
    return call(
        functools.partial(share_kernel, len(terms), pieces),
        (1,),
        [pl.BlockSpec((1, rows, count), lambda i: (0, 0, 0)) for _ in flat],
        pl.BlockSpec(shape, lambda i: (0, 0)),
        jax.ShapeDtypeStruct(shape, F32),
        0,
        4 * rows * count * (len(flat) + len(terms)),
        prefetch=0,
        scratch=[pltpu.VMEM((shape[0], 128), F32)] * 2,
    )(*flat)


def shared_kernel(group, rows, pieces, me_ref, *refs):
    tiles, refs = refs[:group], refs[group:]
    seed_ref, out_ref, high_ref, low_ref, seed_high_ref, seed_low_ref = refs

    @pl.when(pl.program_id(0) == 0)
    def _():
        seed_high_ref[...], seed_low_ref[...] = split(seed_ref[...])

    for g in range(group):
        place = pl.ds(g * rows, rows)
        high_ref[place], low_ref[place] = split(rows_of(tiles[g], rows, pieces))
    total = dot3((high_ref[...], low_ref[...]), (seed_high_ref[...], seed_low_ref[...]))
    for g in range(group):
        out_ref[g] = total[g * rows : (g + 1) * rows]


def shared_products(me, tiles, seed, bits, base, offset, rows, earlier):
    depth, count = seed.shape
    lanes = tiles.shape[2]
    pieces = depth // lanes
    units = 1 << len(bits)
    group = min(units, 4)

    def place(g, f, me_ref):
        return (spread(bits, f * group + g) | base) ^ me_ref[0], offset // rows, 0

    halves = pltpu.VMEM((group * rows, depth), BF16)
    seed_halves = pltpu.VMEM((depth, count), BF16)
    return call(
        functools.partial(shared_kernel, group, rows, pieces),
        (units // group,),
        [
            pl.BlockSpec((1, rows * pieces, lanes), functools.partial(place, g))
            for g in range(group)
        ]
        + [pl.BlockSpec((depth, count), lambda f, me_ref: (0, 0))],
        pl.BlockSpec((group, rows, count), lambda f, me_ref: (f, 0, 0)),
        jax.ShapeDtypeStruct((units, rows, count), F32),
        6 * units * rows * depth * count,
        4 * units * rows * (depth + count),
        scratch=[halves, halves, seed_halves, seed_halves],
        room=34 * MIB,
        earlier=earlier,
    )(me, *([tiles] * group), seed)


def coupled_kernel(units, halves, aliased, last, me_ref, coupling_ref, start_ref, *refs):
    pieces, refs = refs[: units * halves], refs[units * halves :]
    refs = refs[1:] if aliased else refs
    u = pl.program_id(0)
    if last:
        inverse_ref, out_ref, adjoint_ref, second_ref, held_ref, sem = refs
        fetch = pltpu.make_async_copy(inverse_ref, held_ref, sem)
    else:
        second_ref, adjoint_ref, packed_ref = refs

    @pl.when(u == 0)
    def _():
        if last:
            fetch.start()
        second_ref[...] = start_ref[...]

    for g in range(units):

        @pl.when(u == g)
        def _():
            block = jnp.concatenate(
                [ref[...] for ref in pieces[g * halves : (g + 1) * halves]], axis=0
            )
            adjoint_ref[...] = block
            if not last:
                packed_ref[0] = block
            second_ref[...] -= dot(coupling_ref[...], block.astype(BF16))

    if last:

        @pl.when(u == units - 1)
        def _():
            fetch.wait()
            blocks, width, _ = held_ref.shape
            tile = tile_of(width)
            for block in range(blocks):
                second = split(second_ref[block * width : (block + 1) * width])
                for start in range(0, width, tile):
                    out_ref[block, start : start + tile] = dot3(
                        split(held_ref[block, start : start + tile, start:]),
                        [part[start:] for part in second],
                    )


def coupled_step(me, coupling, start, pieces, numbers, adjoint, inverse=None):
    depth, count = start.shape
    halves = len(pieces[0])
    sub = sum(piece.shape[0] for piece in pieces[0])
    units = len(numbers)

    def unit_of(u):
        unit = numbers[-1]
        for g in range(units - 1):
            unit = jnp.where(u == g, numbers[g], unit)
        return unit

    whole = pl.BlockSpec((depth, count), lambda u, me_ref: (0, 0))
    in_specs = [
        pl.BlockSpec((depth, sub), lambda u, me_ref: (0, unit_of(u) ^ me_ref[0])),
        whole,
    ]
    operands = [coupling, start]
    for group in pieces:
        for piece in group:
            in_specs.append(pl.BlockSpec(piece.shape, lambda u, me_ref: (0, 0)))
            operands.append(piece)
    more = {}
    if adjoint is not None:
        in_specs.append(pl.BlockSpec(memory_space=pl.ANY))
        operands.append(adjoint)
        more["input_output_aliases"] = {len(operands): 1}
    flops = 2 * units * depth * sub * count
    moved = units * sub * (2 * depth + 8 * count) + 8 * depth * count
    place = pl.BlockSpec((sub, count), lambda u, me_ref: (unit_of(u) ^ me_ref[0], 0))
    adjoint_shape = jax.ShapeDtypeStruct((coupling.shape[1], count), F32)
    if inverse is None:
        out_specs = [whole, place, pl.BlockSpec((1, sub, count), lambda u, me_ref: (u, 0, 0))]
        out_shape = [
            jax.ShapeDtypeStruct((depth, count), F32),
            adjoint_shape,
            jax.ShapeDtypeStruct((units, sub, count), F32),
        ]
        scratch = ()
    else:
        blocks, width, _ = inverse.shape
        in_specs.append(pl.BlockSpec(memory_space=pl.ANY))
        operands.append(inverse)
        out_specs = [pl.BlockSpec((blocks, width, count), lambda u, me_ref: (0, 0, 0)), place]
        out_shape = [jax.ShapeDtypeStruct((blocks, width, count), F32), adjoint_shape]
        scratch = (
            pltpu.VMEM((depth, count), F32),
            pltpu.VMEM(inverse.shape, F32),
            pltpu.SemaphoreType.DMA(()),
        )
        flops += 6 * inverse.size * count
        moved += 4 * inverse.size
    return call(
        functools.partial(
            coupled_kernel, units, halves, adjoint is not None, inverse is not None
        ),
        (units,),
        in_specs,
        out_specs,
        out_shape,
        flops,
        moved,
        scratch=scratch,
        **more,
    )(me, *operands)


def on_device(scen_count, col_count, private_seeds, private_inverse, coupling, shared_seed, shared_inverse):
    blocks, width = private_inverse.shape[2:4]
    count = private_seeds.shape[4]
    shard_cols = coupling.shape[3]
    sub = shared_seed.shape[1]
    depth = shared_inverse.shape[4]
    devices = scen_count * col_count
    scen_bits, col_bits = scen_count.bit_length() - 1, col_count.bit_length() - 1

    my_scen, my_col = lax.axis_index("scen"), lax.axis_index("col")
    me_scen = my_scen.astype(jnp.int32).reshape(1)
    me = (my_scen * col_count + my_col).astype(jnp.int32).reshape(1)

    def exchange(array, bit):
        return lax.ppermute(array, AXES, [(w, w ^ (1 << bit)) for w in range(devices)])

    flat_coupling = coupling[0].reshape(blocks * width, shard_cols)
    first, half = first_of(private_seeds[0, 0], private_inverse[0, 0])

    def halved(own, arrived, order):
        away, kept = own
        half = away.shape[0]
        terms = [kept, arrived, exchange(away + arrived[half:], order[0])]
        for bit in order[1:]:
            half = terms[-1].shape[0] // 2
            terms.append(exchange(sum(term[half : 2 * half] for term in terms), bit))
        return terms

    core = col_bits
    col_order = list(range(col_bits))
    outer = list(range(core + 1, core + scen_bits))

    orders = [outer, outer[::-1]][: sub // seed_cols(sub)]
    scen_orders = [[bit - core for bit in order] for order in orders]
    arrived = []
    for chunk, order in enumerate(scen_orders):
        away = seed_products(me_scen, flat_coupling, half, sub, [order], 1, chunk * seed_cols(sub))
        arrived.append(exchange(away[0], core))
    own = seed_products(me_scen, flat_coupling, half, sub, scen_orders, 0, 0)
    reduced = reduced_of(
        shared_seed[0],
        [
            halved((kept[kept.shape[0] // 2 :], kept), away, order)
            for kept, away, order in zip(own, arrived, orders)
        ],
    )

    lanes = min(depth, 128)
    tiles = shared_inverse.reshape(devices, sub * depth // lanes, lanes)
    orders = [
        outer + col_order,
        outer[1:] + col_order + outer[:1],
        col_order[:1] + outer + col_order[1:],
        outer + col_order,
    ]
    pieces = depth // lanes
    rows = sub // len(orders)

    def products(chunk, bits, base, *earlier):
        return shared_products(me, tiles, reduced, bits, base, chunk * rows, rows, earlier)

    arrived = [
        exchange(products(chunk, order, 1 << core), core) for chunk, order in enumerate(orders)
    ]
    shares = []
    for chunk, order in enumerate(orders):
        away = products(chunk, order[1:], 1 << order[0], arrived[chunk])
        kept = products(chunk, order[1:], 0, arrived[-1])
        shares.append(halved((away, kept), arrived[chunk], order))

    near = []
    for part, way in enumerate((outer, outer[::-1])):
        held = {0: share_of(shares[2 * part : 2 * part + 2], pieces)}
        for bit in way:
            for number, piece in list(held.items()):
                held[number | (1 << (bit - core))] = exchange(piece, bit)
        near.append(held)
    second, adjoint = first.T, None
    inverse = private_inverse[0, 0]
    numbers = sorted(near[0])
    middle, last = numbers[1:-1], numbers[-1]

    def take(numbers, pieces, inverse=None):
        return coupled_step(me_scen, flat_coupling, second, pieces, numbers, adjoint, inverse)

    own = [held[0] for held in near]
    second, adjoint, _ = take([0, 1], [own, [exchange(piece, core) for piece in own]])
    second, adjoint, packed = take(middle, [[held[number] for held in near] for number in middle])
    far = exchange(packed, core)
    second, adjoint, packed = take([last], [[held[last] for held in near]])
    far_last = exchange(packed, core)
    second, adjoint, _ = take(
        [number | 1 for number in middle], [[far[g]] for g in range(len(middle))]
    )
    second, adjoint = take([last | 1], [[far_last[0]]], inverse)
    return second[None, None], adjoint[None]


def solution(mesh):
    in_specs = (
        P("scen", "col", None, None, None),
        P("scen", "col", None, None, None),
        P("scen", None, None, "col"),
        P("col", "scen", None),
        P(None, None, None, "col", "scen"),
    )
    out_specs = (P("scen", "col", None, None, None), P("col", None, None))
    return jax.shard_map(
        functools.partial(on_device, mesh.shape["scen"], mesh.shape["col"]),
        mesh=mesh,
        in_specs=in_specs,
        out_specs=out_specs,
        check_vma=False,
    )
```

```python
import functools
import math

import jax
import jax.numpy as jnp
from jax import lax
from jax.experimental import pallas as pl
from jax.experimental.pallas import tpu as pltpu
from jax.sharding import PartitionSpec as P

F32, BF16 = jnp.float32, jnp.bfloat16
AXES = ("scen", "col")
MIB = 1024 * 1024


def split(value):
    high = value.astype(BF16)
    return high, (value - high.astype(F32)).astype(BF16)


def dot(left, right):
    return jnp.dot(left, right, preferred_element_type=F32)


def dot3(left, right):
    (left_high, left_low), (right_high, right_low) = left, right
    return dot(left_high, right_high) + (dot(left_low, right_high) + dot(left_high, right_low))


def tile_of(width):
    return 256 if width % 256 == 0 else width


def bytes_of(spec, dtype):
    shape = spec.block_shape
    return 0 if shape is None else math.prod(shape) * dtype.itemsize


def call(kernel, grid, in_specs, out_specs, out_shape, flops, moved, prefetch=1, scratch=(), room=None, earlier=(), **more):
    inputs = prefetch + len(in_specs)
    body = kernel
    if earlier:
        body = lambda *refs: kernel(*refs[:inputs], *refs[inputs + len(earlier) :])
    in_specs = list(in_specs) + [pl.BlockSpec(memory_space=pl.ANY)] * len(earlier)

    def run(*operands):
        operands += tuple(earlier)
        outs = out_shape if isinstance(out_shape, (list, tuple)) else [out_shape]
        specs = out_specs if isinstance(out_specs, (list, tuple)) else [out_specs]
        need = sum(2 * bytes_of(s, o.dtype) for s, o in zip(in_specs, operands[prefetch:]))
        need += sum(2 * bytes_of(s, o.dtype) for s, o in zip(specs, outs))
        need += sum(
            math.prod(s.shape) * jnp.dtype(s.dtype).itemsize for s in scratch if len(s.shape) > 1
        )
        return pl.pallas_call(
            body,
            grid_spec=pltpu.PrefetchScalarGridSpec(
                num_scalar_prefetch=prefetch,
                grid=grid,
                in_specs=in_specs,
                out_specs=out_specs,
                scratch_shapes=list(scratch),
            ),
            out_shape=out_shape,
            compiler_params=pltpu.CompilerParams(vmem_limit_bytes=room or need + 10 * MIB),
            cost_estimate=pl.CostEstimate(
                flops=int(flops) // 1, bytes_accessed=int(moved) // 1, transcendentals=0
            ),
            **more,
        )(*operands)

    return run


def spread(bits, place):
    unit = 0
    for j, bit in enumerate(bits):
        unit = unit | (((place >> (len(bits) - 1 - j)) & 1) << bit)
    return unit


def place_of(bits, unit):
    place = 0
    for bit in bits:
        place = place * 2 + ((unit >> bit) & 1)
    return place


def first_kernel(seeds_ref, inverse_ref, first_ref, half_ref):
    width = inverse_ref.shape[1]
    tile = tile_of(width)
    seeds = split(seeds_ref[0].T)
    inverse = split(inverse_ref[0])
    for start in range(0, width, tile):
        stop = start + tile
        first = dot3(
            [part[:, :stop] for part in seeds], [part[:stop, start:stop] for part in inverse]
        )
        first_ref[:, start:stop] = first
        half_ref[:, start:stop] = first.astype(BF16)


def first_of(seeds, inverse):
    blocks, width, count = seeds.shape
    across = pl.BlockSpec((count, width), lambda b: (0, b))
    return call(
        first_kernel,
        (blocks,),
        [
            pl.BlockSpec((1, width, count), lambda b: (b, 0, 0)),
            pl.BlockSpec((1, width, width), lambda b: (b, 0, 0)),
        ],
        [across, across],
        [
            jax.ShapeDtypeStruct((count, blocks * width), F32),
            jax.ShapeDtypeStruct((count, blocks * width), BF16),
        ],
        6 * blocks * width * width * count,
        4 * blocks * width * (width + 3 * count),
        prefetch=0,
    )(seeds, inverse)


def seed_kernel(me_ref, coupling_ref, half_ref, *sum_refs):
    total = dot(half_ref[...], coupling_ref[...])
    cols = total.shape[1] // len(sum_refs)
    for chunk, ref in enumerate(sum_refs):
        ref[0] = total[:, chunk * cols : (chunk + 1) * cols]


def seed_products(me, coupling, half, sub, orders, base, offset):
    count, depth = half.shape
    cols = seed_cols(sub)
    wide = cols * len(orders)
    units = 1 << len(orders[0])

    def unit_of(f):
        return spread(orders[0], f) | base

    return call(
        seed_kernel,
        (units,),
        [
            pl.BlockSpec(
                (depth, wide), lambda f, me_ref: (0, ((unit_of(f) ^ me_ref[0]) * sub + offset) // wide)
            ),
            pl.BlockSpec((count, depth), lambda f, me_ref: (0, 0)),
        ],
        [
            pl.BlockSpec(
                (1, count, cols),
                functools.partial(
                    lambda order, f, me_ref: (place_of(order, unit_of(f)), 0, 0), order
                ),
            )
            for order in orders
        ],
        [jax.ShapeDtypeStruct((units, count, cols), F32)] * len(orders),
        2 * units * depth * wide * count,
        units * wide * (2 * depth + 4 * count),
    )(me, coupling, half)


def seed_cols(sub):
    return sub // 2 if sub % 256 == 0 else sub


def reduced_kernel(chunks, seed_ref, *refs):
    *terms, out_ref = refs
    each = len(terms) // chunks
    cols = terms[0].shape[2]
    for chunk in range(chunks):
        place = pl.ds(chunk * cols, cols)
        total = sum(ref[0] for ref in terms[chunk * each : (chunk + 1) * each])
        out_ref[place] = seed_ref[place] - total.T


def reduced_of(seed, terms):
    whole = pl.BlockSpec(seed.shape, lambda i: (0, 0))
    flat = [term for chunk in terms for term in chunk]
    return call(
        functools.partial(reduced_kernel, len(terms)),
        (1,),
        [whole] + [pl.BlockSpec((1, *term.shape[1:]), lambda i: (0, 0, 0)) for term in flat],
        whole,
        jax.ShapeDtypeStruct(seed.shape, F32),
        0,
        16 * seed.size,
        prefetch=0,
        room=40 * MIB,
    )(seed, *flat)


def rows_of(tile_ref, rows, pieces):
    if pieces == 1:
        return tile_ref[0]
    lanes = tile_ref.shape[2]
    parts = tile_ref[0].reshape(rows // 8, pieces, 8, lanes)
    parts = [parts[:, j] for j in range(pieces)]
    at = lax.broadcasted_iota(jnp.int32, (rows // 8, 8, lanes), 1)
    step = 1
    while step < pieces:
        upper = (at & step) != 0
        for j in range(pieces):
            if j & step == 0:
                low, high = parts[j], parts[j + step]
                parts[j] = jnp.where(upper, pltpu.roll(high, step, 1), low)
                parts[j + step] = jnp.where(upper, high, pltpu.roll(low, 8 - step, 1))
        step *= 2
    return jnp.concatenate([part.reshape(rows, lanes) for part in parts], axis=1)


def share_kernel(chunks, pieces, *refs):
    terms, out_ref, held_ref, order_ref = refs[:-3], *refs[-3:]
    each = len(terms) // chunks
    rows = terms[0].shape[1]
    run = 8 // pieces
    total = jnp.concatenate(
        [sum(ref[0] for ref in terms[at : at + each]) for at in range(0, len(terms), each)], axis=0
    )
    for lane in range(0, total.shape[1], 128):
        held_ref[...] = total[:, lane : lane + 128]
        for place in range(8):
            j, b = place // run, place % run
            order_ref[pl.ds(place, chunks * rows // 8, stride=8), :] = held_ref[
                pl.ds(b * pieces + j, chunks * rows // 8, stride=8), :
            ]
        out_ref[:, lane : lane + 128] = order_ref[...]


def share_of(terms, pieces):
    _, rows, count = terms[0][0].shape
    flat = [term for chunk in terms for term in chunk]
    shape = (len(terms) * rows, count)
    return call(
        functools.partial(share_kernel, len(terms), pieces),
        (1,),
        [pl.BlockSpec((1, rows, count), lambda i: (0, 0, 0)) for _ in flat],
        pl.BlockSpec(shape, lambda i: (0, 0)),
        jax.ShapeDtypeStruct(shape, F32),
        0,
        4 * rows * count * (len(flat) + len(terms)),
        prefetch=0,
        scratch=[pltpu.VMEM((shape[0], 128), F32)] * 2,
    )(*flat)


def shared_kernel(group, rows, pieces, arrived, me_ref, *refs):
    tiles, refs = refs[:group], refs[group:]
    seed_ref, *received, out_ref, parts_ref, seed_parts_ref = refs
    depth = seed_ref.shape[0]

    @pl.when(pl.program_id(0) == 0)
    def _():
        high, low = split(seed_ref[...])
        seed_parts_ref[:depth] = high
        seed_parts_ref[depth : 2 * depth] = high
        seed_parts_ref[2 * depth :] = low

    for g in range(group):
        place = pl.ds(g * rows, rows)
        high, low = split(rows_of(tiles[g], rows, pieces))
        parts_ref[place, :depth] = high
        parts_ref[place, depth : 2 * depth] = low
        parts_ref[place, 2 * depth :] = high
    total = dot(parts_ref[...], seed_parts_ref[...])
    for g in range(group):
        term = total[g * rows : (g + 1) * rows]
        out_ref[g] = term + received[0][g] if arrived else term


def shared_products(me, tiles, seed, bits, base, offset, rows, received=None, earlier=()):
    depth, count = seed.shape
    lanes = tiles.shape[2]
    pieces = depth // lanes
    units = 1 << len(bits)
    group = min(units, 4)

    def place(g, f, me_ref):
        return (spread(bits, f * group + g) | base) ^ me_ref[0], offset // rows, 0

    in_specs = [
        pl.BlockSpec((1, rows * pieces, lanes), functools.partial(place, g)) for g in range(group)
    ] + [pl.BlockSpec((depth, count), lambda f, me_ref: (0, 0))]
    operands = [tiles] * group + [seed]
    if received is not None:
        skip = received.shape[0] // group - units // group
        in_specs.append(pl.BlockSpec((group, rows, count), lambda f, me_ref: (skip + f, 0, 0)))
        operands.append(received)
    return call(
        functools.partial(shared_kernel, group, rows, pieces, received is not None),
        (units // group,),
        in_specs,
        pl.BlockSpec((group, rows, count), lambda f, me_ref: (f, 0, 0)),
        jax.ShapeDtypeStruct((units, rows, count), F32),
        6 * units * rows * depth * count,
        4 * units * rows * (depth + count),
        scratch=[pltpu.VMEM((group * rows, 3 * depth), BF16), pltpu.VMEM((3 * depth, count), BF16)],
        room=34 * MIB,
        earlier=earlier,
    )(me, *operands)


def coupled_kernel(units, halves, aliased, last, me_ref, coupling_ref, start_ref, *refs):
    pieces, refs = refs[: units * halves], refs[units * halves :]
    refs = refs[1:] if aliased else refs
    u = pl.program_id(0)
    if last:
        inverse_ref, out_ref, adjoint_ref, second_ref, held_ref, sem = refs
        fetch = pltpu.make_async_copy(inverse_ref, held_ref, sem)
    else:
        second_ref, adjoint_ref, packed_ref = refs

    @pl.when(u == 0)
    def _():
        if last:
            fetch.start()
        second_ref[...] = start_ref[...]

    for g in range(units):

        @pl.when(u == g)
        def _():
            block = jnp.concatenate(
                [ref[...] for ref in pieces[g * halves : (g + 1) * halves]], axis=0
            )
            adjoint_ref[...] = block
            if not last:
                packed_ref[0] = block
            second_ref[...] -= dot(coupling_ref[...], block.astype(BF16))

    if last:

        @pl.when(u == units - 1)
        def _():
            fetch.wait()
            blocks, width, _ = held_ref.shape
            tile = tile_of(width)
            for block in range(blocks):
                second = split(second_ref[block * width : (block + 1) * width])
                for start in range(0, width, tile):
                    out_ref[block, start : start + tile] = dot3(
                        split(held_ref[block, start : start + tile, start:]),
                        [part[start:] for part in second],
                    )


def coupled_step(me, coupling, start, pieces, numbers, adjoint, inverse=None):
    depth, count = start.shape
    halves = len(pieces[0])
    sub = sum(piece.shape[0] for piece in pieces[0])
    units = len(numbers)

    def unit_of(u):
        unit = numbers[-1]
        for g in range(units - 1):
            unit = jnp.where(u == g, numbers[g], unit)
        return unit

    whole = pl.BlockSpec((depth, count), lambda u, me_ref: (0, 0))
    in_specs = [
        pl.BlockSpec((depth, sub), lambda u, me_ref: (0, unit_of(u) ^ me_ref[0])),
        whole,
    ]
    operands = [coupling, start]
    for group in pieces:
        for piece in group:
            in_specs.append(pl.BlockSpec(piece.shape, lambda u, me_ref: (0, 0)))
            operands.append(piece)
    more = {}
    if adjoint is not None:
        in_specs.append(pl.BlockSpec(memory_space=pl.ANY))
        operands.append(adjoint)
        more["input_output_aliases"] = {len(operands): 1}
    flops = 2 * units * depth * sub * count
    moved = units * sub * (2 * depth + 8 * count) + 8 * depth * count
    place = pl.BlockSpec((sub, count), lambda u, me_ref: (unit_of(u) ^ me_ref[0], 0))
    adjoint_shape = jax.ShapeDtypeStruct((coupling.shape[1], count), F32)
    if inverse is None:
        out_specs = [whole, place, pl.BlockSpec((1, sub, count), lambda u, me_ref: (u, 0, 0))]
        out_shape = [
            jax.ShapeDtypeStruct((depth, count), F32),
            adjoint_shape,
            jax.ShapeDtypeStruct((units, sub, count), F32),
        ]
        scratch = ()
    else:
        blocks, width, _ = inverse.shape
        in_specs.append(pl.BlockSpec(memory_space=pl.ANY))
        operands.append(inverse)
        out_specs = [pl.BlockSpec((blocks, width, count), lambda u, me_ref: (0, 0, 0)), place]
        out_shape = [jax.ShapeDtypeStruct((blocks, width, count), F32), adjoint_shape]
        scratch = (
            pltpu.VMEM((depth, count), F32),
            pltpu.VMEM(inverse.shape, F32),
            pltpu.SemaphoreType.DMA(()),
        )
        flops += 6 * inverse.size * count
        moved += 4 * inverse.size
    return call(
        functools.partial(
            coupled_kernel, units, halves, adjoint is not None, inverse is not None
        ),
        (units,),
        in_specs,
        out_specs,
        out_shape,
        flops,
        moved,
        scratch=scratch,
        room=52 * MIB,
        **more,
    )(me, *operands)


def on_device(scen_count, col_count, private_seeds, private_inverse, coupling, shared_seed, shared_inverse):
    blocks, width = private_inverse.shape[2:4]
    count = private_seeds.shape[4]
    shard_cols = coupling.shape[3]
    sub = shared_seed.shape[1]
    depth = shared_inverse.shape[4]
    devices = scen_count * col_count
    scen_bits, col_bits = scen_count.bit_length() - 1, col_count.bit_length() - 1

    my_scen, my_col = lax.axis_index("scen"), lax.axis_index("col")
    me_scen = my_scen.astype(jnp.int32).reshape(1)
    me = (my_scen * col_count + my_col).astype(jnp.int32).reshape(1)

    def exchange(array, bit):
        return lax.ppermute(array, AXES, [(w, w ^ (1 << bit)) for w in range(devices)])

    flat_coupling = coupling[0].reshape(blocks * width, shard_cols)
    first, half = first_of(private_seeds[0, 0], private_inverse[0, 0])

    def halved(away, terms, order):
        for step, bit in enumerate(order):
            if step > 0:
                half = terms[-1].shape[0] // 2
                away = sum(term[half : 2 * half] for term in terms)
            terms = terms + [exchange(away, bit)]
        return terms

    core = col_bits
    col_order = list(range(col_bits))
    outer = list(range(core + 1, core + scen_bits))

    orders = [outer, outer[::-1]][: sub // seed_cols(sub)]
    scen_orders = [[bit - core for bit in order] for order in orders]
    arrived = []
    for chunk, order in enumerate(scen_orders):
        away = seed_products(me_scen, flat_coupling, half, sub, [order], 1, chunk * seed_cols(sub))
        arrived.append(exchange(away[0], core))
    own = seed_products(me_scen, flat_coupling, half, sub, scen_orders, 0, 0)
    reduced = reduced_of(
        shared_seed[0],
        [
            halved(sum(term[term.shape[0] // 2 :] for term in pair), list(pair), order)
            for *pair, order in zip(own, arrived, orders)
        ],
    )

    lanes = min(depth, 128)
    tiles = shared_inverse.reshape(devices, sub * depth // lanes, lanes)
    orders = [
        outer + col_order,
        outer[1:] + col_order + outer[:1],
        col_order[:1] + outer + col_order[1:],
        outer + col_order,
    ]
    pieces = depth // lanes
    rows = sub // len(orders)

    def products(chunk, base, received=None, earlier=()):
        bits = orders[chunk] if base == 1 << core else orders[chunk][1:]
        return shared_products(
            me, tiles, reduced, bits, base, chunk * rows, rows, received, earlier
        )

    arrived = [exchange(products(chunk, 1 << core), core) for chunk in range(len(orders))]
    away = [
        products(chunk, 1 << order[0], arrived[chunk]) for chunk, order in enumerate(orders)
    ]
    shares = []
    for chunk, order in enumerate(orders):
        kept = products(chunk, 0, earlier=away)
        shares.append(halved(away[chunk], [kept, arrived[chunk]], order))

    near = []
    for part, way in enumerate((outer, outer[::-1])):
        held = {0: share_of(shares[2 * part : 2 * part + 2], pieces)}
        for bit in way:
            for number, piece in list(held.items()):
                held[number | (1 << (bit - core))] = exchange(piece, bit)
        near.append(held)
    second, adjoint = first.T, None
    inverse = private_inverse[0, 0]
    numbers = sorted(near[0])
    middle, last = numbers[1:-1], numbers[-1]

    def take(numbers, pieces, inverse=None):
        return coupled_step(me_scen, flat_coupling, second, pieces, numbers, adjoint, inverse)

    own = [held[0] for held in near]
    second, adjoint, _ = take([0, 1], [own, [exchange(piece, core) for piece in own]])
    far = [[exchange(held[number], core) for held in near] for number in middle]
    second, adjoint, _ = take(middle, [[held[number] for held in near] for number in middle])
    second, adjoint, packed = take([last], [[held[last] for held in near]])
    far_last = exchange(packed, core)
    second, adjoint, _ = take([number | 1 for number in middle], far)
    second, adjoint = take([last | 1], [[far_last[0]]], inverse)
    return second[None, None], adjoint[None]


def solution(mesh):
    in_specs = (
        P("scen", "col", None, None, None),
        P("scen", "col", None, None, None),
        P("scen", None, None, "col"),
        P("col", "scen", None),
        P(None, None, None, "col", "scen"),
    )
    out_specs = (P("scen", "col", None, None, None), P("col", None, None))
    return jax.shard_map(
        functools.partial(on_device, mesh.shape["scen"], mesh.shape["col"]),
        mesh=mesh,
        in_specs=in_specs,
        out_specs=out_specs,
        check_vma=False,
    )
```

```python
import functools
import math

import jax
import jax.numpy as jnp
from jax import lax
from jax.experimental import pallas as pl
from jax.experimental.pallas import tpu as pltpu
from jax.sharding import PartitionSpec as P

F32, BF16 = jnp.float32, jnp.bfloat16
AXES = ("scen", "col")
MIB = 1024 * 1024


def split(value):
    high = value.astype(BF16)
    return high, (value - high.astype(F32)).astype(BF16)


def dot(left, right):
    return jnp.dot(left, right, preferred_element_type=F32)


def dot3(left, right):
    (left_high, left_low), (right_high, right_low) = left, right
    return dot(left_high, right_high) + (dot(left_low, right_high) + dot(left_high, right_low))


def tile_of(width):
    return 256 if width % 256 == 0 else width


def bytes_of(spec, dtype):
    shape = spec.block_shape
    return 0 if shape is None else math.prod(shape) * dtype.itemsize


def call(kernel, grid, in_specs, out_specs, out_shape, flops, moved, prefetch=1, scratch=(), room=None, earlier=(), **more):
    inputs = prefetch + len(in_specs)
    body = kernel
    if earlier:
        body = lambda *refs: kernel(*refs[:inputs], *refs[inputs + len(earlier) :])
    in_specs = list(in_specs) + [pl.BlockSpec(memory_space=pl.ANY)] * len(earlier)

    def run(*operands):
        operands += tuple(earlier)
        outs = out_shape if isinstance(out_shape, (list, tuple)) else [out_shape]
        specs = out_specs if isinstance(out_specs, (list, tuple)) else [out_specs]
        need = sum(2 * bytes_of(s, o.dtype) for s, o in zip(in_specs, operands[prefetch:]))
        need += sum(2 * bytes_of(s, o.dtype) for s, o in zip(specs, outs))
        need += sum(
            math.prod(s.shape) * jnp.dtype(s.dtype).itemsize for s in scratch if len(s.shape) > 1
        )
        return pl.pallas_call(
            body,
            grid_spec=pltpu.PrefetchScalarGridSpec(
                num_scalar_prefetch=prefetch,
                grid=grid,
                in_specs=in_specs,
                out_specs=out_specs,
                scratch_shapes=list(scratch),
            ),
            out_shape=out_shape,
            compiler_params=pltpu.CompilerParams(vmem_limit_bytes=room or need + 10 * MIB),
            cost_estimate=pl.CostEstimate(
                flops=int(flops) // 1, bytes_accessed=int(moved) // 1, transcendentals=0
            ),
            **more,
        )(*operands)

    return run


def spread(bits, place):
    unit = 0
    for j, bit in enumerate(bits):
        unit = unit | (((place >> (len(bits) - 1 - j)) & 1) << bit)
    return unit


def place_of(bits, unit):
    place = 0
    for bit in bits:
        place = place * 2 + ((unit >> bit) & 1)
    return place


def upper_tiles(count):
    return [(i, j) for i in range(count) for j in range(i, count)]


def first_kernel(parts, *refs):
    seeds_refs, inverse_refs, (first_ref, half_ref) = refs[:parts], refs[parts:-2], refs[-2:]
    tile = seeds_refs[0].shape[1]
    seeds = [split(ref[0].T) for ref in seeds_refs]
    firsts = [None] * parts
    for (i, j), ref in zip(upper_tiles(parts), inverse_refs):
        term = dot3(seeds[i], split(ref[0]))
        firsts[j] = term if i == 0 else firsts[j] + term
    for j, first in enumerate(firsts):
        first_ref[:, j * tile : (j + 1) * tile] = first
        half_ref[:, j * tile : (j + 1) * tile] = first.astype(BF16)


def first_of(seeds, inverse):
    blocks, width, count = seeds.shape
    tile = tile_of(width)
    parts = width // tile
    across = pl.BlockSpec((count, width), lambda b: (0, b))
    return call(
        functools.partial(first_kernel, parts),
        (blocks,),
        [
            pl.BlockSpec((1, tile, count), functools.partial(lambda i, b: (b, i, 0), i))
            for i in range(parts)
        ]
        + [
            pl.BlockSpec((1, tile, tile), functools.partial(lambda i, j, b: (b, i, j), i, j))
            for i, j in upper_tiles(parts)
        ],
        [across, across],
        [
            jax.ShapeDtypeStruct((count, blocks * width), F32),
            jax.ShapeDtypeStruct((count, blocks * width), BF16),
        ],
        6 * blocks * width * width * count,
        4 * blocks * width * (width + 3 * count),
        prefetch=0,
        room=58 * MIB,
    )(*([seeds] * parts), *([inverse] * len(upper_tiles(parts))))


def seed_kernel(strips, me_ref, *refs):
    coupling_refs, half_ref, sum_refs = refs[:strips], refs[strips], refs[strips + 1 :]
    depth = coupling_refs[0].shape[0]
    total = sum(
        dot(half_ref[:, at * depth : (at + 1) * depth], ref[...])
        for at, ref in enumerate(coupling_refs)
    )
    cols = total.shape[1] // len(sum_refs)
    for chunk, ref in enumerate(sum_refs):
        ref[0] = total[:, chunk * cols : (chunk + 1) * cols]


def seed_products(me, coupling, half, sub, orders, base, offset):
    count, depth = half.shape
    cols = seed_cols(sub)
    wide = cols * len(orders)
    units = 1 << len(orders[0])

    def unit_of(f):
        return spread(orders[0], f) | base

    def place(strip, f, me_ref):
        return strip, ((unit_of(f) ^ me_ref[0]) * sub + offset) // wide

    strip = strip_of(depth)
    strips = depth // strip
    return call(
        functools.partial(seed_kernel, strips),
        (units,),
        [
            pl.BlockSpec((strip, wide), functools.partial(place, number))
            for number in range(strips)
        ]
        + [
            pl.BlockSpec((count, depth), lambda f, me_ref: (0, 0)),
        ],
        [
            pl.BlockSpec(
                (1, count, cols),
                functools.partial(
                    lambda order, f, me_ref: (place_of(order, unit_of(f)), 0, 0), order
                ),
            )
            for order in orders
        ],
        [jax.ShapeDtypeStruct((units, count, cols), F32)] * len(orders),
        2 * units * depth * wide * count,
        units * wide * (2 * depth + 4 * count),
        room=52 * MIB,
    )(me, *([coupling] * strips), half)


def strip_of(depth):
    return 256 if depth % 256 == 0 else depth


def seed_cols(sub):
    return sub // 2 if sub % 256 == 0 else sub


def reduced_kernel(chunks, seed_ref, *refs):
    *terms, out_ref = refs
    each = len(terms) // chunks
    cols = terms[0].shape[2]
    for chunk in range(chunks):
        place = pl.ds(chunk * cols, cols)
        total = sum(ref[0] for ref in terms[chunk * each : (chunk + 1) * each])
        out_ref[place] = seed_ref[place] - total.T


def reduced_of(seed, terms):
    whole = pl.BlockSpec(seed.shape, lambda i: (0, 0))
    flat = [term for chunk in terms for term in chunk]
    return call(
        functools.partial(reduced_kernel, len(terms)),
        (1,),
        [whole] + [pl.BlockSpec((1, *term.shape[1:]), lambda i: (0, 0, 0)) for term in flat],
        whole,
        jax.ShapeDtypeStruct(seed.shape, F32),
        0,
        16 * seed.size,
        prefetch=0,
    )(seed, *flat)


def rows_of(tile_ref, rows, pieces):
    if pieces == 1:
        return tile_ref[0]
    lanes = tile_ref.shape[2]
    parts = tile_ref[0].reshape(rows // 8, pieces, 8, lanes)
    parts = [parts[:, j] for j in range(pieces)]
    at = lax.broadcasted_iota(jnp.int32, (rows // 8, 8, lanes), 1)
    step = 1
    while step < pieces:
        upper = (at & step) != 0
        for j in range(pieces):
            if j & step == 0:
                low, high = parts[j], parts[j + step]
                parts[j] = jnp.where(upper, pltpu.roll(high, step, 1), low)
                parts[j + step] = jnp.where(upper, high, pltpu.roll(low, 8 - step, 1))
        step *= 2
    return jnp.concatenate([part.reshape(rows, lanes) for part in parts], axis=1)


def share_kernel(chunks, pieces, *refs):
    terms, out_ref, held_ref, order_ref = refs[:-3], *refs[-3:]
    each = len(terms) // chunks
    rows = terms[0].shape[1]
    run = 8 // pieces
    total = jnp.concatenate(
        [sum(ref[0] for ref in terms[at : at + each]) for at in range(0, len(terms), each)], axis=0
    )
    for lane in range(0, total.shape[1], 128):
        held_ref[...] = total[:, lane : lane + 128]
        for place in range(8):
            j, b = place // run, place % run
            order_ref[pl.ds(place, chunks * rows // 8, stride=8), :] = held_ref[
                pl.ds(b * pieces + j, chunks * rows // 8, stride=8), :
            ]
        out_ref[:, lane : lane + 128] = order_ref[...]


def share_of(terms, pieces):
    _, rows, count = terms[0][0].shape
    flat = [term for chunk in terms for term in chunk]
    shape = (len(terms) * rows, count)
    return call(
        functools.partial(share_kernel, len(terms), pieces),
        (1,),
        [pl.BlockSpec((1, rows, count), lambda i: (0, 0, 0)) for _ in flat],
        pl.BlockSpec(shape, lambda i: (0, 0)),
        jax.ShapeDtypeStruct(shape, F32),
        0,
        4 * rows * count * (len(flat) + len(terms)),
        prefetch=0,
        scratch=[pltpu.VMEM((shape[0], 128), F32)] * 2,
    )(*flat)


def shared_kernel(group, strips, pieces, arrived, me_ref, *refs):
    tiles, refs = refs[: group * strips], refs[group * strips :]
    seed_ref, *received, out_ref, parts_ref, seed_parts_ref = refs
    depth = seed_ref.shape[0]
    rows = parts_ref.shape[0] // group
    strip = rows // strips

    @pl.when(pl.program_id(0) == 0)
    def _():
        high, low = split(seed_ref[...])
        seed_parts_ref[:depth] = high
        seed_parts_ref[depth : 2 * depth] = high
        seed_parts_ref[2 * depth :] = low

    for at, ref in enumerate(tiles):
        place = pl.ds(at * strip, strip)
        high, low = split(rows_of(ref, strip, pieces))
        parts_ref[place, :depth] = high
        parts_ref[place, depth : 2 * depth] = low
        parts_ref[place, 2 * depth :] = high
    total = dot(parts_ref[...], seed_parts_ref[...])
    for g in range(group):
        term = total[g * rows : (g + 1) * rows]
        out_ref[g] = term + received[0][g] if arrived else term


def shared_products(me, tiles, seed, bits, base, offset, rows, received=None, earlier=()):
    depth, count = seed.shape
    lanes = tiles.shape[2]
    pieces = depth // lanes
    units = 1 << len(bits)
    group = min(units, 4)
    strips = next(n for n in (4, 2, 1) if rows % (n * 16) == 0 or n == 1)

    def place(g, strip, f, me_ref):
        unit = (spread(bits, f * group + g) | base) ^ me_ref[0]
        return unit, offset // rows * strips + strip, 0

    in_specs = [
        pl.BlockSpec((1, rows // strips * pieces, lanes), functools.partial(place, g, strip))
        for g in range(group)
        for strip in range(strips)
    ] + [pl.BlockSpec((depth, count), lambda f, me_ref: (0, 0))]
    operands = [tiles] * (group * strips) + [seed]
    if received is not None:
        skip = received.shape[0] // group - units // group
        in_specs.append(pl.BlockSpec((group, rows, count), lambda f, me_ref: (skip + f, 0, 0)))
        operands.append(received)
    return call(
        functools.partial(shared_kernel, group, strips, pieces, received is not None),
        (units // group,),
        in_specs,
        pl.BlockSpec((group, rows, count), lambda f, me_ref: (f, 0, 0)),
        jax.ShapeDtypeStruct((units, rows, count), F32),
        6 * units * rows * depth * count,
        4 * units * rows * (depth + count),
        scratch=[pltpu.VMEM((group * rows, 3 * depth), BF16), pltpu.VMEM((3 * depth, count), BF16)],
        room=34 * MIB,
        earlier=earlier,
    )(me, *operands)


def coupled_kernel(units, halves, strips, aliased, last, me_ref, *refs):
    coupling_refs, start_ref, refs = refs[:strips], refs[strips], refs[strips + 1 :]
    pieces, refs = refs[: units * halves], refs[units * halves :]
    refs = refs[1:] if aliased else refs
    u = pl.program_id(0)
    if last:
        inverse_ref, out_ref, adjoint_ref, second_ref, held_ref, sems = refs
        blocks, width, _ = inverse_ref.shape
        tile = held_ref.shape[2]
        parts = width // tile
        places = [(block, i, j) for block in range(blocks) for i, j in upper_tiles(parts)]
        fetches = [
            pltpu.make_async_copy(
                inverse_ref.at[block, pl.ds(i * tile, tile), pl.ds(j * tile, tile)],
                held_ref.at[at],
                sems.at[at],
            )
            for at, (block, i, j) in enumerate(places)
        ]
    else:
        second_ref, adjoint_ref, packed_ref = refs

    @pl.when(u == 0)
    def _():
        if last:
            for fetch in fetches:
                fetch.start()
        second_ref[...] = start_ref[...]

    for g in range(units):

        @pl.when(u == g)
        def _():
            block = jnp.concatenate(
                [ref[...] for ref in pieces[g * halves : (g + 1) * halves]], axis=0
            )
            adjoint_ref[...] = block
            if not last:
                packed_ref[0] = block
            half = block.astype(BF16)
            for at, ref in enumerate(coupling_refs):
                place = pl.ds(at * ref.shape[0], ref.shape[0])
                second_ref[place] -= dot(ref[...], half)

    if last:

        @pl.when(u == units - 1)
        def _():
            second = [
                split(second_ref[at * tile : (at + 1) * tile]) for at in range(blocks * parts)
            ]
            totals = {}
            for at, (block, i, j) in enumerate(places):
                fetches[at].wait()
                term = dot3(split(held_ref[at]), second[block * parts + j])
                totals[block, i] = term if i == j else totals[block, i] + term
            for (block, i), total in totals.items():
                out_ref[block, i * tile : (i + 1) * tile] = total


def coupled_step(me, coupling, start, pieces, numbers, adjoint, inverse=None):
    depth, count = start.shape
    halves = len(pieces[0])
    sub = sum(piece.shape[0] for piece in pieces[0])
    units = len(numbers)

    def unit_of(u):
        unit = numbers[-1]
        for g in range(units - 1):
            unit = jnp.where(u == g, numbers[g], unit)
        return unit

    whole = pl.BlockSpec((depth, count), lambda u, me_ref: (0, 0))
    strip = strip_of(depth)
    strips = depth // strip
    in_specs = [
        pl.BlockSpec(
            (strip, sub), functools.partial(lambda at, u, me_ref: (at, unit_of(u) ^ me_ref[0]), at)
        )
        for at in range(strips)
    ] + [whole]
    operands = [coupling] * strips + [start]
    for group in pieces:
        for piece in group:
            in_specs.append(pl.BlockSpec(piece.shape, lambda u, me_ref: (0, 0)))
            operands.append(piece)
    more = {}
    if adjoint is not None:
        in_specs.append(pl.BlockSpec(memory_space=pl.ANY))
        operands.append(adjoint)
        more["input_output_aliases"] = {len(operands): 1}
    flops = 2 * units * depth * sub * count
    moved = units * sub * (2 * depth + 8 * count) + 8 * depth * count
    place = pl.BlockSpec((sub, count), lambda u, me_ref: (unit_of(u) ^ me_ref[0], 0))
    adjoint_shape = jax.ShapeDtypeStruct((coupling.shape[1], count), F32)
    if inverse is None:
        out_specs = [whole, place, pl.BlockSpec((1, sub, count), lambda u, me_ref: (u, 0, 0))]
        out_shape = [
            jax.ShapeDtypeStruct((depth, count), F32),
            adjoint_shape,
            jax.ShapeDtypeStruct((units, sub, count), F32),
        ]
        scratch = ()
    else:
        blocks, width, _ = inverse.shape
        tiles = blocks * len(upper_tiles(width // tile_of(width)))
        in_specs.append(pl.BlockSpec(memory_space=pl.ANY))
        operands.append(inverse)
        out_specs = [pl.BlockSpec((blocks, width, count), lambda u, me_ref: (0, 0, 0)), place]
        out_shape = [jax.ShapeDtypeStruct((blocks, width, count), F32), adjoint_shape]
        scratch = (
            pltpu.VMEM((depth, count), F32),
            pltpu.VMEM((tiles, tile_of(width), tile_of(width)), F32),
            pltpu.SemaphoreType.DMA((tiles,)),
        )
        flops += 6 * inverse.size * count
        moved += 4 * inverse.size
    return call(
        functools.partial(
            coupled_kernel, units, halves, strips, adjoint is not None, inverse is not None
        ),
        (units,),
        in_specs,
        out_specs,
        out_shape,
        flops,
        moved,
        scratch=scratch,
        room=52 * MIB,
        **more,
    )(me, *operands)


def on_device(scen_count, col_count, private_seeds, private_inverse, coupling, shared_seed, shared_inverse):
    blocks, width = private_inverse.shape[2:4]
    count = private_seeds.shape[4]
    shard_cols = coupling.shape[3]
    sub = shared_seed.shape[1]
    depth = shared_inverse.shape[4]
    devices = scen_count * col_count
    scen_bits, col_bits = scen_count.bit_length() - 1, col_count.bit_length() - 1

    my_scen, my_col = lax.axis_index("scen"), lax.axis_index("col")
    me_scen = my_scen.astype(jnp.int32).reshape(1)
    me = (my_scen * col_count + my_col).astype(jnp.int32).reshape(1)

    def exchange(array, bit):
        return lax.ppermute(array, AXES, [(w, w ^ (1 << bit)) for w in range(devices)])

    flat_coupling = coupling[0].reshape(blocks * width, shard_cols)
    first, half = first_of(private_seeds[0, 0], private_inverse[0, 0])

    def halved(away, terms, order):
        for step, bit in enumerate(order):
            if step > 0:
                half = terms[-1].shape[0] // 2
                away = sum(term[half : 2 * half] for term in terms)
            terms = terms + [exchange(away, bit)]
        return terms

    core = col_bits
    col_order = list(range(col_bits))
    outer = list(range(core + 1, core + scen_bits))

    orders = [outer, outer[::-1]][: sub // seed_cols(sub)]
    scen_orders = [[bit - core for bit in order] for order in orders]
    arrived = []
    for chunk, order in enumerate(scen_orders):
        away = seed_products(me_scen, flat_coupling, half, sub, [order], 1, chunk * seed_cols(sub))
        arrived.append(exchange(away[0], core))
    own = seed_products(me_scen, flat_coupling, half, sub, scen_orders, 0, 0)
    reduced = reduced_of(
        shared_seed[0],
        [
            [sum(term[:1] for term in terms[:-1]), terms[-1]]
            for terms in (
                halved(sum(term[term.shape[0] // 2 :] for term in pair), list(pair), order)
                for *pair, order in zip(own, arrived, orders)
            )
        ],
    )

    lanes = min(depth, 128)
    tiles = shared_inverse.reshape(devices, sub * depth // lanes, lanes)
    orders = [
        outer + col_order,
        outer[1:] + col_order + outer[:1],
        col_order[:1] + outer + col_order[1:],
        outer + col_order,
    ]
    pieces = depth // lanes
    rows = sub // len(orders)

    def products(chunk, base, received=None, earlier=()):
        bits = orders[chunk] if base == 1 << core else orders[chunk][1:]
        return shared_products(
            me, tiles, reduced, bits, base, chunk * rows, rows, received, earlier
        )

    arrived = [exchange(products(chunk, 1 << core), core) for chunk in range(len(orders))]
    away = [
        products(chunk, 1 << order[0], arrived[chunk]) for chunk, order in enumerate(orders)
    ]
    shares = []
    for chunk, order in enumerate(orders):
        kept = products(chunk, 0, earlier=away)
        shares.append(halved(away[chunk], [kept, arrived[chunk]], order))

    near = []
    for part, way in enumerate((outer, outer[::-1])):
        held = {0: share_of(shares[2 * part : 2 * part + 2], pieces)}
        for bit in way:
            for number, piece in list(held.items()):
                held[number | (1 << (bit - core))] = exchange(piece, bit)
        near.append(held)
    second, adjoint = first.T, None
    inverse = private_inverse[0, 0]
    numbers = sorted(near[0])
    middle, last = numbers[1:-1], numbers[-1]

    def take(numbers, pieces, inverse=None):
        return coupled_step(me_scen, flat_coupling, second, pieces, numbers, adjoint, inverse)

    own = [held[0] for held in near]
    second, adjoint, _ = take([0, 1], [own, [exchange(piece, core) for piece in own]])
    far = [[exchange(held[number], core) for held in near] for number in middle]
    second, adjoint, _ = take(middle, [[held[number] for held in near] for number in middle])
    second, adjoint, packed = take([last], [[held[last] for held in near]])
    far_last = exchange(packed, core)
    second, adjoint, _ = take([number | 1 for number in middle], far)
    second, adjoint = take([last | 1], [[far_last[0]]], inverse)
    return second[None, None], adjoint[None]


def solution(mesh):
    in_specs = (
        P("scen", "col", None, None, None),
        P("scen", "col", None, None, None),
        P("scen", None, None, "col"),
        P("col", "scen", None),
        P(None, None, None, "col", "scen"),
    )
    out_specs = (P("scen", "col", None, None, None), P("col", None, None))
    return jax.shard_map(
        functools.partial(on_device, mesh.shape["scen"], mesh.shape["col"]),
        mesh=mesh,
        in_specs=in_specs,
        out_specs=out_specs,
        check_vma=False,
    )
```

```python
import functools
import math

import jax
import jax.numpy as jnp
from jax import lax
from jax.experimental import pallas as pl
from jax.experimental.pallas import tpu as pltpu
from jax.sharding import PartitionSpec as P

F32, BF16 = jnp.float32, jnp.bfloat16
AXES = ("scen", "col")
MIB = 1024 * 1024


def split(value):
    high = value.astype(BF16)
    return high, (value - high.astype(F32)).astype(BF16)


def dot(left, right):
    return jnp.dot(left, right, preferred_element_type=F32)


def dot3(left, right):
    (left_high, left_low), (right_high, right_low) = left, right
    return dot(left_high, right_high) + (dot(left_low, right_high) + dot(left_high, right_low))


def tile_of(width):
    return 256 if width % 256 == 0 else width


def bytes_of(spec, dtype):
    shape = spec.block_shape
    return 0 if shape is None else math.prod(shape) * dtype.itemsize


def call(kernel, grid, in_specs, out_specs, out_shape, flops, moved, prefetch=1, scratch=(), room=None, earlier=(), **more):
    inputs = prefetch + len(in_specs)
    body = kernel
    if earlier:
        body = lambda *refs: kernel(*refs[:inputs], *refs[inputs + len(earlier) :])
    in_specs = list(in_specs) + [pl.BlockSpec(memory_space=pl.ANY)] * len(earlier)

    def run(*operands):
        operands += tuple(earlier)
        outs = out_shape if isinstance(out_shape, (list, tuple)) else [out_shape]
        specs = out_specs if isinstance(out_specs, (list, tuple)) else [out_specs]
        need = sum(2 * bytes_of(s, o.dtype) for s, o in zip(in_specs, operands[prefetch:]))
        need += sum(2 * bytes_of(s, o.dtype) for s, o in zip(specs, outs))
        need += sum(
            math.prod(s.shape) * jnp.dtype(s.dtype).itemsize for s in scratch if len(s.shape) > 1
        )
        return pl.pallas_call(
            body,
            grid_spec=pltpu.PrefetchScalarGridSpec(
                num_scalar_prefetch=prefetch,
                grid=grid,
                in_specs=in_specs,
                out_specs=out_specs,
                scratch_shapes=list(scratch),
            ),
            out_shape=out_shape,
            compiler_params=pltpu.CompilerParams(vmem_limit_bytes=room or need + 10 * MIB),
            cost_estimate=pl.CostEstimate(
                flops=int(flops) // 1, bytes_accessed=int(moved) // 1, transcendentals=0
            ),
            **more,
        )(*operands)

    return run


def spread(bits, place):
    unit = 0
    for j, bit in enumerate(bits):
        unit = unit | (((place >> (len(bits) - 1 - j)) & 1) << bit)
    return unit


def place_of(bits, unit):
    place = 0
    for bit in bits:
        place = place * 2 + ((unit >> bit) & 1)
    return place


def upper_tiles(count):
    return [(i, j) for i in range(count) for j in range(i, count)]


def first_kernel(parts, *refs):
    seeds_refs, inverse_refs, (first_ref, half_ref) = refs[:parts], refs[parts:-2], refs[-2:]
    tile = seeds_refs[0].shape[1]
    seeds = [split(ref[0].T) for ref in seeds_refs]
    firsts = [None] * parts
    for (i, j), ref in zip(upper_tiles(parts), inverse_refs):
        term = dot3(seeds[i], split(ref[0]))
        firsts[j] = term if i == 0 else firsts[j] + term
    for j, first in enumerate(firsts):
        first_ref[:, j * tile : (j + 1) * tile] = first
        half_ref[:, j * tile : (j + 1) * tile] = first.astype(BF16)


def first_of(seeds, inverse):
    blocks, width, count = seeds.shape
    tile = tile_of(width)
    parts = width // tile
    across = pl.BlockSpec((count, width), lambda b: (0, b))
    return call(
        functools.partial(first_kernel, parts),
        (blocks,),
        [
            pl.BlockSpec((1, tile, count), functools.partial(lambda i, b: (b, i, 0), i))
            for i in range(parts)
        ]
        + [
            pl.BlockSpec((1, tile, tile), functools.partial(lambda i, j, b: (b, i, j), i, j))
            for i, j in upper_tiles(parts)
        ],
        [across, across],
        [
            jax.ShapeDtypeStruct((count, blocks * width), F32),
            jax.ShapeDtypeStruct((count, blocks * width), BF16),
        ],
        6 * blocks * width * width * count,
        4 * blocks * width * (width + 3 * count),
        prefetch=0,
        room=58 * MIB,
    )(*([seeds] * parts), *([inverse] * len(upper_tiles(parts))))


def seed_kernel(strips, me_ref, *refs):
    coupling_refs, half_ref, sum_refs = refs[:strips], refs[strips], refs[strips + 1 :]
    depth = coupling_refs[0].shape[0]
    total = sum(
        dot(half_ref[:, at * depth : (at + 1) * depth], ref[...])
        for at, ref in enumerate(coupling_refs)
    )
    cols = total.shape[1] // len(sum_refs)
    for chunk, ref in enumerate(sum_refs):
        ref[0] = total[:, chunk * cols : (chunk + 1) * cols]


def seed_products(me, coupling, half, sub, orders, base, offset):
    count, depth = half.shape
    cols = seed_cols(sub)
    wide = cols * len(orders)
    units = 1 << len(orders[0])

    def unit_of(f):
        return spread(orders[0], f) | base

    def place(strip, f, me_ref):
        return strip, ((unit_of(f) ^ me_ref[0]) * sub + offset) // wide

    strip = strip_of(depth)
    strips = depth // strip
    return call(
        functools.partial(seed_kernel, strips),
        (units,),
        [
            pl.BlockSpec((strip, wide), functools.partial(place, number))
            for number in range(strips)
        ]
        + [
            pl.BlockSpec((count, depth), lambda f, me_ref: (0, 0)),
        ],
        [
            pl.BlockSpec(
                (1, count, cols),
                functools.partial(
                    lambda order, f, me_ref: (place_of(order, unit_of(f)), 0, 0), order
                ),
            )
            for order in orders
        ],
        [jax.ShapeDtypeStruct((units, count, cols), F32)] * len(orders),
        2 * units * depth * wide * count,
        units * wide * (2 * depth + 4 * count),
        room=52 * MIB,
    )(me, *([coupling] * strips), half)


def strip_of(depth):
    return 256 if depth % 256 == 0 else depth


def seed_cols(sub):
    return sub // 2 if sub % 256 == 0 else sub


def reduced_kernel(chunks, seed_ref, *refs):
    *terms, out_ref = refs
    each = len(terms) // chunks
    cols = terms[0].shape[2]
    for chunk in range(chunks):
        place = pl.ds(chunk * cols, cols)
        total = sum(ref[0] for ref in terms[chunk * each : (chunk + 1) * each])
        out_ref[place] = seed_ref[place] - total.T


def reduced_of(seed, terms):
    whole = pl.BlockSpec(seed.shape, lambda i: (0, 0))
    flat = [term for chunk in terms for term in chunk]
    return call(
        functools.partial(reduced_kernel, len(terms)),
        (1,),
        [whole] + [pl.BlockSpec((1, *term.shape[1:]), lambda i: (0, 0, 0)) for term in flat],
        whole,
        jax.ShapeDtypeStruct(seed.shape, F32),
        0,
        16 * seed.size,
        prefetch=0,
    )(seed, *flat)


def share_kernel(chunks, *refs):
    *terms, out_ref = refs
    each = len(terms) // chunks
    rows = terms[0].shape[1]
    for chunk in range(chunks):
        out_ref[chunk * rows : (chunk + 1) * rows] = sum(
            ref[0] for ref in terms[chunk * each : (chunk + 1) * each]
        )


def share_of(terms):
    _, rows, count = terms[0][0].shape
    flat = [term for chunk in terms for term in chunk]
    shape = (len(terms) * rows, count)
    return call(
        functools.partial(share_kernel, len(terms)),
        (1,),
        [pl.BlockSpec((1, rows, count), lambda i: (0, 0, 0)) for _ in flat],
        pl.BlockSpec(shape, lambda i: (0, 0)),
        jax.ShapeDtypeStruct(shape, F32),
        0,
        4 * rows * count * (len(flat) + len(terms)),
        prefetch=0,
    )(*flat)


def shared_kernel(bits, inner, base, col_bits, pieces, me_ref, *refs):
    tiles, refs = refs[:pieces], refs[pieces:]
    seed_ref, *received, out_ref, parts_ref, seed_parts_ref = refs
    depth = seed_ref.shape[0]
    group = 1 << len(inner)
    rows = parts_ref.shape[0] // group
    lanes = depth // pieces
    step = pl.program_id(0)

    @pl.when(step == 0)
    def _():
        high, low = split(seed_ref[...])
        seed_parts_ref[:depth] = high
        seed_parts_ref[depth : 2 * depth] = high
        seed_parts_ref[2 * depth :] = low

    for piece, ref in enumerate(tiles):
        high, low = split(ref.reshape(group * rows, lanes)[...])
        at = piece * lanes
        parts_ref[:, at : at + lanes] = high
        parts_ref[:, depth + at : depth + at + lanes] = low
        parts_ref[:, 2 * depth + at : 2 * depth + at + lanes] = high
    total = dot(parts_ref[...], seed_parts_ref[...])
    outer_bits = [bit for bit in bits if bit not in inner]
    for g in range(group):
        unit = spread(outer_bits, step) | (spread(inner, g) ^ (me_ref[0] & spread(inner, group - 1)))
        place = place_of(bits, unit)
        term = total[g * rows : (g + 1) * rows]
        if received:
            term = term + received[0][place]
        out_ref[place] = term


def shared_products(me, tiles, seed, bits, base, offset, rows, received=None, earlier=()):
    depth, count = seed.shape
    lanes = min(depth, 128)
    pieces = depth // lanes
    col_bits = tiles.ndim - 4
    units = 1 << len(bits)
    inner = sorted([bit for bit in bits if bit < col_bits], reverse=True)
    outer_bits = [bit for bit in bits if bit >= col_bits]
    group = 1 << len(inner)

    def place(piece, f, me_ref):
        unit = (spread(outer_bits, f) | base) ^ me_ref[0]
        cols = [0 if bit in inner else (unit >> bit) & 1 for bit in reversed(range(col_bits))]
        return (unit >> col_bits, *cols, offset // rows, 0, piece)

    block = [2 if bit in inner else 1 for bit in reversed(range(col_bits))]
    in_specs = [
        pl.BlockSpec((1, *block, rows, 1, lanes), functools.partial(place, piece))
        for piece in range(pieces)
    ] + [pl.BlockSpec((depth, count), lambda f, me_ref: (0, 0))]
    operands = [tiles] * pieces + [seed]
    if received is not None:
        half = received.shape[0] // units - 1
        in_specs.append(pl.BlockSpec((units, rows, count), lambda f, me_ref: (half, 0, 0)))
        operands.append(received)
    return call(
        functools.partial(shared_kernel, bits, inner, base, col_bits, pieces),
        (units // group,),
        in_specs,
        pl.BlockSpec((units, rows, count), lambda f, me_ref: (0, 0, 0)),
        jax.ShapeDtypeStruct((units, rows, count), F32),
        6 * units * rows * depth * count,
        4 * units * rows * (depth + count),
        scratch=[pltpu.VMEM((group * rows, 3 * depth), BF16), pltpu.VMEM((3 * depth, count), BF16)],
        room=34 * MIB,
        earlier=earlier,
    )(me, *operands)


def coupled_kernel(counts, strips, aliased, packs, last, me_ref, *refs):
    coupling_refs, start_ref, refs = refs[:strips], refs[strips], refs[strips + 1 :]
    units, given = len(counts), sum(counts)
    pieces, refs = refs[:given], refs[given:]
    refs = refs[1:] if aliased else refs
    u = pl.program_id(0)
    if last:
        inverse_ref, out_ref, adjoint_ref, second_ref, held_ref, sems = refs
        blocks, width, _ = inverse_ref.shape
        tile = held_ref.shape[2]
        parts = width // tile
        places = [(block, i, j) for block in range(blocks) for i, j in upper_tiles(parts)]
        fetches = [
            pltpu.make_async_copy(
                inverse_ref.at[block, pl.ds(i * tile, tile), pl.ds(j * tile, tile)],
                held_ref.at[at],
                sems.at[at],
            )
            for at, (block, i, j) in enumerate(places)
        ]
    else:
        second_ref, adjoint_ref = refs[:2]

    @pl.when(u == 0)
    def _():
        if last:
            for fetch in fetches:
                fetch.start()
        second_ref[...] = start_ref[...] if aliased else start_ref[...].T

    for g in range(units):

        @pl.when(u == g)
        def _():
            begin = sum(counts[:g])
            block = [ref[...] for ref in pieces[begin : begin + counts[g]]]
            block = block[0] if len(block) == 1 else jnp.concatenate(block, axis=0)
            adjoint_ref[...] = block
            if packs:
                refs[2][0] = block
            half = block.astype(BF16)
            for at, ref in enumerate(coupling_refs):
                place = pl.ds(at * ref.shape[0], ref.shape[0])
                second_ref[place] -= dot(ref[...], half)

    if last:

        @pl.when(u == units - 1)
        def _():
            second = [
                split(second_ref[at * tile : (at + 1) * tile]) for at in range(blocks * parts)
            ]
            totals = {}
            for at, (block, i, j) in enumerate(places):
                fetches[at].wait()
                term = dot3(split(held_ref[at]), second[block * parts + j])
                totals[block, i] = term if i == j else totals[block, i] + term
            for (block, i), total in totals.items():
                out_ref[block, i * tile : (i + 1) * tile] = total


def coupled_step(me, coupling, start, pieces, numbers, adjoint, packs=False, inverse=None):
    depth, count = coupling.shape[0], pieces[0][0].shape[1]
    sub = sum(piece.shape[0] for piece in pieces[0])
    units = len(numbers)

    def unit_of(u):
        unit = numbers[-1]
        for g in range(units - 1):
            unit = jnp.where(u == g, numbers[g], unit)
        return unit

    whole = pl.BlockSpec((depth, count), lambda u, me_ref: (0, 0))
    strip = strip_of(depth)
    strips = depth // strip
    in_specs = [
        pl.BlockSpec(
            (strip, sub), functools.partial(lambda at, u, me_ref: (at, unit_of(u) ^ me_ref[0]), at)
        )
        for at in range(strips)
    ] + [pl.BlockSpec(start.shape, lambda u, me_ref: (0, 0))]
    operands = [coupling] * strips + [start]
    for group in pieces:
        for piece in group:
            in_specs.append(pl.BlockSpec(piece.shape, lambda u, me_ref: (0, 0)))
            operands.append(piece)
    more = {}
    if adjoint is not None:
        in_specs.append(pl.BlockSpec(memory_space=pl.ANY))
        operands.append(adjoint)
        more["input_output_aliases"] = {len(operands): 1}
    flops = 2 * units * depth * sub * count
    moved = units * sub * (2 * depth + 8 * count) + 8 * depth * count
    place = pl.BlockSpec((sub, count), lambda u, me_ref: (unit_of(u) ^ me_ref[0], 0))
    adjoint_shape = jax.ShapeDtypeStruct((coupling.shape[1], count), F32)
    if inverse is None:
        out_specs = [whole, place]
        out_shape = [jax.ShapeDtypeStruct((depth, count), F32), adjoint_shape]
        if packs:
            out_specs.append(pl.BlockSpec((1, sub, count), lambda u, me_ref: (u, 0, 0)))
            out_shape.append(jax.ShapeDtypeStruct((units, sub, count), F32))
        scratch = ()
    else:
        blocks, width, _ = inverse.shape
        tiles = blocks * len(upper_tiles(width // tile_of(width)))
        in_specs.append(pl.BlockSpec(memory_space=pl.ANY))
        operands.append(inverse)
        out_specs = [pl.BlockSpec((blocks, width, count), lambda u, me_ref: (0, 0, 0)), place]
        out_shape = [jax.ShapeDtypeStruct((blocks, width, count), F32), adjoint_shape]
        scratch = (
            pltpu.VMEM((depth, count), F32),
            pltpu.VMEM((tiles, tile_of(width), tile_of(width)), F32),
            pltpu.SemaphoreType.DMA((tiles,)),
        )
        flops += 6 * inverse.size * count
        moved += 4 * inverse.size
    return call(
        functools.partial(
            coupled_kernel,
            tuple(len(group) for group in pieces),
            strips,
            adjoint is not None,
            packs,
            inverse is not None,
        ),
        (units,),
        in_specs,
        out_specs,
        out_shape,
        flops,
        moved,
        scratch=scratch,
        room=52 * MIB,
        **more,
    )(me, *operands)


def on_device(scen_count, col_count, private_seeds, private_inverse, coupling, shared_seed, shared_inverse):
    blocks, width = private_inverse.shape[2:4]
    count = private_seeds.shape[4]
    shard_cols = coupling.shape[3]
    sub = shared_seed.shape[1]
    depth = shared_inverse.shape[4]
    devices = scen_count * col_count
    scen_bits, col_bits = scen_count.bit_length() - 1, col_count.bit_length() - 1

    my_scen, my_col = lax.axis_index("scen"), lax.axis_index("col")
    me_scen = my_scen.astype(jnp.int32).reshape(1)
    me = (my_scen * col_count + my_col).astype(jnp.int32).reshape(1)

    def exchange(array, bit):
        return lax.ppermute(array, AXES, [(w, w ^ (1 << bit)) for w in range(devices)])

    flat_coupling = coupling[0].reshape(blocks * width, shard_cols)
    first, half = first_of(private_seeds[0, 0], private_inverse[0, 0])

    def halved(away, terms, order):
        for step, bit in enumerate(order):
            if step > 0:
                half = terms[-1].shape[0] // 2
                away = sum(term[half : 2 * half] for term in terms)
            terms = terms + [exchange(away, bit)]
        return terms

    core = col_bits
    col_order = list(range(col_bits))
    outer = list(range(core + 1, core + scen_bits))

    orders = [outer, outer[::-1]][: sub // seed_cols(sub)]
    scen_orders = [[bit - core for bit in order] for order in orders]
    arrived = []
    for chunk, order in enumerate(scen_orders):
        away = seed_products(me_scen, flat_coupling, half, sub, [order], 1, chunk * seed_cols(sub))
        arrived.append(exchange(away[0], core))
    own = seed_products(me_scen, flat_coupling, half, sub, scen_orders, 0, 0)
    reduced = reduced_of(
        shared_seed[0],
        [
            [sum(term[:1] for term in terms[:-1]), terms[-1]]
            for terms in (
                halved(sum(term[term.shape[0] // 2 :] for term in pair), list(pair), order)
                for *pair, order in zip(own, arrived, orders)
            )
        ],
    )

    tiles = shared_inverse.reshape(scen_count, *([2] * col_bits), sub, 1, depth)
    orders = [
        outer + col_order,
        outer[1:] + col_order + outer[:1],
        col_order[:1] + outer + col_order[1:],
        outer + col_order,
    ]
    rows = sub // len(orders)

    def products(chunk, base, received=None, earlier=()):
        bits = orders[chunk] if base == 1 << core else orders[chunk][1:]
        return shared_products(
            me, tiles, reduced, bits, base, chunk * rows, rows, received, earlier
        )

    arrived = [exchange(products(chunk, 1 << core), core) for chunk in range(len(orders))]
    away = [
        products(chunk, 1 << order[0], arrived[chunk]) for chunk, order in enumerate(orders)
    ]
    shares = []
    for chunk, order in enumerate(orders):
        kept = products(chunk, 0, earlier=away)
        shares.append(halved(away[chunk], [kept, arrived[chunk]], order))

    near = []
    for part, way in enumerate((outer, outer[::-1])):
        held = {0: share_of(shares[2 * part : 2 * part + 2])}
        for bit in way:
            for number, piece in list(held.items()):
                held[number | (1 << (bit - core))] = exchange(piece, bit)
        near.append(held)
    inverse = private_inverse[0, 0]
    numbers = sorted(near[0])
    middle, last = numbers[1:-1], numbers[-1]
    own = [held[0] for held in near]
    across = [exchange(piece, core) for piece in own]
    far = [[exchange(held[number], core) for held in near] for number in middle]
    second, adjoint = coupled_step(
        me_scen,
        flat_coupling,
        first,
        [own, across] + [[held[number] for held in near] for number in middle],
        [0, 1] + middle,
        None,
    )
    second, adjoint, packed = coupled_step(
        me_scen, flat_coupling, second, [[held[last] for held in near]], [last], adjoint, packs=True
    )
    packed = exchange(packed, core).reshape(sub, count)
    second, adjoint = coupled_step(
        me_scen,
        flat_coupling,
        second,
        far + [[packed]],
        [number | 1 for number in middle + [last]],
        adjoint,
        inverse=inverse,
    )
    return second[None, None], adjoint[None]


def solution(mesh):
    in_specs = (
        P("scen", "col", None, None, None),
        P("scen", "col", None, None, None),
        P("scen", None, None, "col"),
        P("col", "scen", None),
        P(None, None, None, "col", "scen"),
    )
    out_specs = (P("scen", "col", None, None, None), P("col", None, None))
    return jax.shard_map(
        functools.partial(on_device, mesh.shape["scen"], mesh.shape["col"]),
        mesh=mesh,
        in_specs=in_specs,
        out_specs=out_specs,
        check_vma=False,
    )
```

```python
import functools
import math

import jax
import jax.numpy as jnp
from jax import lax
from jax.experimental import pallas as pl
from jax.experimental.pallas import tpu as pltpu
from jax.sharding import PartitionSpec as P

F32, BF16 = jnp.float32, jnp.bfloat16
AXES = ("scen", "col")
MIB = 1024 * 1024


def split(value):
    high = value.astype(BF16)
    return high, (value - high.astype(F32)).astype(BF16)


def dot(left, right):
    return jnp.dot(left, right, preferred_element_type=F32)


def dot3(left, right):
    (left_high, left_low), (right_high, right_low) = left, right
    return dot(left_high, right_high) + (dot(left_low, right_high) + dot(left_high, right_low))


def tile_of(width):
    return 256 if width % 256 == 0 else width


def bytes_of(spec, dtype):
    shape = spec.block_shape
    return 0 if shape is None else math.prod(shape) * dtype.itemsize


def call(kernel, grid, in_specs, out_specs, out_shape, flops, moved, prefetch=1, scratch=(), room=None, earlier=(), **more):
    inputs = prefetch + len(in_specs)
    body = kernel
    if earlier:
        body = lambda *refs: kernel(*refs[:inputs], *refs[inputs + len(earlier) :])
    in_specs = list(in_specs) + [pl.BlockSpec(memory_space=pl.ANY)] * len(earlier)

    def run(*operands):
        operands += tuple(earlier)
        outs = out_shape if isinstance(out_shape, (list, tuple)) else [out_shape]
        specs = out_specs if isinstance(out_specs, (list, tuple)) else [out_specs]
        need = sum(2 * bytes_of(s, o.dtype) for s, o in zip(in_specs, operands[prefetch:]))
        need += sum(2 * bytes_of(s, o.dtype) for s, o in zip(specs, outs))
        need += sum(
            math.prod(s.shape) * jnp.dtype(s.dtype).itemsize for s in scratch if len(s.shape) > 1
        )
        return pl.pallas_call(
            body,
            grid_spec=pltpu.PrefetchScalarGridSpec(
                num_scalar_prefetch=prefetch,
                grid=grid,
                in_specs=in_specs,
                out_specs=out_specs,
                scratch_shapes=list(scratch),
            ),
            out_shape=out_shape,
            compiler_params=pltpu.CompilerParams(vmem_limit_bytes=room or need + 10 * MIB),
            cost_estimate=pl.CostEstimate(
                flops=int(flops) // 1, bytes_accessed=int(moved) // 1, transcendentals=0
            ),
            **more,
        )(*operands)

    return run


def spread(bits, place):
    unit = 0
    for j, bit in enumerate(bits):
        unit = unit | (((place >> (len(bits) - 1 - j)) & 1) << bit)
    return unit


def place_of(bits, unit):
    place = 0
    for bit in bits:
        place = place * 2 + ((unit >> bit) & 1)
    return place


def upper_tiles(count):
    return [(i, j) for i in range(count) for j in range(i, count)]


def first_kernel(parts, *refs):
    seeds_refs, inverse_refs, (first_ref, half_ref) = refs[:parts], refs[parts:-2], refs[-2:]
    tile = seeds_refs[0].shape[1]
    seeds = [split(ref[0].T) for ref in seeds_refs]
    firsts = [None] * parts
    for (i, j), ref in zip(upper_tiles(parts), inverse_refs):
        term = dot3(seeds[i], split(ref[0]))
        firsts[j] = term if i == 0 else firsts[j] + term
    for j, first in enumerate(firsts):
        first_ref[:, j * tile : (j + 1) * tile] = first
        half_ref[:, j * tile : (j + 1) * tile] = first.astype(BF16)


def first_of(seeds, inverse):
    blocks, width, count = seeds.shape
    tile = tile_of(width)
    parts = width // tile
    across = pl.BlockSpec((count, width), lambda b: (0, b))
    return call(
        functools.partial(first_kernel, parts),
        (blocks,),
        [
            pl.BlockSpec((1, tile, count), functools.partial(lambda i, b: (b, i, 0), i))
            for i in range(parts)
        ]
        + [
            pl.BlockSpec((1, tile, tile), functools.partial(lambda i, j, b: (b, i, j), i, j))
            for i, j in upper_tiles(parts)
        ],
        [across, across],
        [
            jax.ShapeDtypeStruct((count, blocks * width), F32),
            jax.ShapeDtypeStruct((count, blocks * width), BF16),
        ],
        6 * blocks * width * width * count,
        4 * blocks * width * (width + 3 * count),
        prefetch=0,
        room=58 * MIB,
    )(*([seeds] * parts), *([inverse] * len(upper_tiles(parts))))


def seed_kernel(pair, strips, orders, base, me_ref, *refs):
    coupling_refs, half_ref = refs[: pair * strips], refs[pair * strips]
    sum_refs = refs[pair * strips + 1 :]
    depth = coupling_refs[0].shape[0]
    cols = sum_refs[0].shape[2]
    for g in range(pair):
        unit = spread(orders[0], pl.program_id(0) * pair + g)
        total = sum(
            dot(half_ref[:, at * depth : (at + 1) * depth], coupling_refs[g * strips + at][...])
            for at in range(strips)
        )
        for chunk, (order, ref) in enumerate(zip(orders, sum_refs)):
            ref[place_of(order, unit)] = total[:, chunk * cols : (chunk + 1) * cols]


def seed_products(me, coupling, half, sub, orders, base, offset):
    count, depth = half.shape
    cols = seed_cols(sub)
    wide = cols * len(orders)
    units = 1 << len(orders[0])
    pair = min(units, 2)
    strip = strip_of(depth)
    strips = depth // strip

    def place(g, strip, f, me_ref):
        unit = spread(orders[0], f * pair + g) | base
        return strip, ((unit ^ me_ref[0]) * sub + offset) // wide

    return call(
        functools.partial(seed_kernel, pair, strips, orders, base),
        (units // pair,),
        [
            pl.BlockSpec((strip, wide), functools.partial(place, g, number))
            for g in range(pair)
            for number in range(strips)
        ]
        + [pl.BlockSpec((count, depth), lambda f, me_ref: (0, 0))],
        [pl.BlockSpec((units, count, cols), lambda f, me_ref: (0, 0, 0))] * len(orders),
        [jax.ShapeDtypeStruct((units, count, cols), F32)] * len(orders),
        2 * units * depth * wide * count,
        units * wide * (2 * depth + 4 * count),
        room=52 * MIB,
    )(me, *([coupling] * (pair * strips)), half)


def strip_of(depth):
    return 256 if depth % 256 == 0 else depth


def seed_cols(sub):
    return sub // 2 if sub % 256 == 0 else sub


def reduced_kernel(chunks, seed_ref, *refs):
    *terms, out_ref = refs
    each = len(terms) // chunks
    cols = terms[0].shape[2]
    for chunk in range(chunks):
        place = pl.ds(chunk * cols, cols)
        total = sum(ref[0] for ref in terms[chunk * each : (chunk + 1) * each])
        out_ref[place] = seed_ref[place] - total.T


def reduced_of(seed, terms):
    whole = pl.BlockSpec(seed.shape, lambda i: (0, 0))
    flat = [term for chunk in terms for term in chunk]
    return call(
        functools.partial(reduced_kernel, len(terms)),
        (1,),
        [whole] + [pl.BlockSpec((1, *term.shape[1:]), lambda i: (0, 0, 0)) for term in flat],
        whole,
        jax.ShapeDtypeStruct(seed.shape, F32),
        0,
        16 * seed.size,
        prefetch=0,
    )(seed, *flat)


def share_kernel(chunks, *refs):
    *terms, out_ref = refs
    each = len(terms) // chunks
    rows = terms[0].shape[1]
    for chunk in range(chunks):
        out_ref[chunk * rows : (chunk + 1) * rows] = sum(
            ref[0] for ref in terms[chunk * each : (chunk + 1) * each]
        )


def share_of(terms):
    _, rows, count = terms[0][0].shape
    flat = [term for chunk in terms for term in chunk]
    shape = (len(terms) * rows, count)
    return call(
        functools.partial(share_kernel, len(terms)),
        (1,),
        [pl.BlockSpec((1, rows, count), lambda i: (0, 0, 0)) for _ in flat],
        pl.BlockSpec(shape, lambda i: (0, 0)),
        jax.ShapeDtypeStruct(shape, F32),
        0,
        4 * rows * count * (len(flat) + len(terms)),
        prefetch=0,
    )(*flat)


def shared_kernel(bits, inner, several, pieces, me_ref, *refs):
    tiles, refs = refs[: several * pieces], refs[several * pieces :]
    seed_ref, *received, out_ref, parts_ref, seed_parts_ref = refs
    depth = seed_ref.shape[0]
    group = 1 << len(inner)
    rows = parts_ref.shape[0] // (group * several)
    lanes = depth // pieces
    step = pl.program_id(0)

    @pl.when(step == 0)
    def _():
        high, low = split(seed_ref[...])
        seed_parts_ref[:depth] = high
        seed_parts_ref[depth : 2 * depth] = high
        seed_parts_ref[2 * depth :] = low

    for number, ref in enumerate(tiles):
        high, low = split(ref.reshape(group * rows, lanes)[...])
        at, place = number % pieces * lanes, pl.ds(number // pieces * group * rows, group * rows)
        parts_ref[place, at : at + lanes] = high
        parts_ref[place, depth + at : depth + at + lanes] = low
        parts_ref[place, 2 * depth + at : 2 * depth + at + lanes] = high
    total = dot(parts_ref[...], seed_parts_ref[...])
    outer_bits = [bit for bit in bits if bit not in inner]
    for g in range(several * group):
        col = spread(inner, g % group) ^ (me_ref[0] & spread(inner, group - 1))
        unit = spread(outer_bits, step * several + g // group) | col
        place = place_of(bits, unit)
        term = total[g * rows : (g + 1) * rows]
        if received:
            term = term + received[0][place]
        out_ref[place] = term


def shared_products(me, tiles, seed, bits, base, offset, rows, received=None, earlier=()):
    depth, count = seed.shape
    lanes = min(depth, 128)
    pieces = depth // lanes
    col_bits = tiles.ndim - 4
    units = 1 << len(bits)
    inner = sorted([bit for bit in bits if bit < col_bits], reverse=True)
    outer_bits = [bit for bit in bits if bit >= col_bits]
    group = 1 << len(inner)
    several = 1

    def place(number, piece, f, me_ref):
        unit = (spread(outer_bits, f * several + number) | base) ^ me_ref[0]
        cols = [0 if bit in inner else (unit >> bit) & 1 for bit in reversed(range(col_bits))]
        return (unit >> col_bits, *cols, offset // rows, 0, piece)

    block = [2 if bit in inner else 1 for bit in reversed(range(col_bits))]
    in_specs = [
        pl.BlockSpec((1, *block, rows, 1, lanes), functools.partial(place, number, piece))
        for number in range(several)
        for piece in range(pieces)
    ] + [pl.BlockSpec((depth, count), lambda f, me_ref: (0, 0))]
    operands = [tiles] * (several * pieces) + [seed]
    if received is not None:
        half = received.shape[0] // units - 1
        in_specs.append(pl.BlockSpec((units, rows, count), lambda f, me_ref: (half, 0, 0)))
        operands.append(received)
    return call(
        functools.partial(shared_kernel, bits, inner, several, pieces),
        (units // (group * several),),
        in_specs,
        pl.BlockSpec((units, rows, count), lambda f, me_ref: (0, 0, 0)),
        jax.ShapeDtypeStruct((units, rows, count), F32),
        6 * units * rows * depth * count,
        4 * units * rows * (depth + count),
        scratch=[
            pltpu.VMEM((several * group * rows, 3 * depth), BF16),
            pltpu.VMEM((3 * depth, count), BF16),
        ],
        room=34 * MIB,
        earlier=earlier,
    )(me, *operands)


def coupled_kernel(counts, strips, aliased, packs, last, me_ref, *refs):
    coupling_refs, start_ref, refs = refs[:strips], refs[strips], refs[strips + 1 :]
    units, given = len(counts), sum(counts)
    pieces, refs = refs[:given], refs[given:]
    refs = refs[1:] if aliased else refs
    u = pl.program_id(0)
    if last:
        inverse_ref, out_ref, adjoint_ref, second_ref, held_ref, sems = refs
        blocks, width, _ = inverse_ref.shape
        tile = held_ref.shape[2]
        parts = width // tile
        places = [(block, i, j) for block in range(blocks) for i, j in upper_tiles(parts)]
        fetches = [
            pltpu.make_async_copy(
                inverse_ref.at[block, pl.ds(i * tile, tile), pl.ds(j * tile, tile)],
                held_ref.at[at],
                sems.at[at],
            )
            for at, (block, i, j) in enumerate(places)
        ]
    else:
        second_ref, adjoint_ref = refs[:2]

    @pl.when(u == 0)
    def _():
        if last:
            for fetch in fetches:
                fetch.start()
        second_ref[...] = start_ref[...] if aliased else start_ref[...].T

    for g in range(units):

        @pl.when(u == g)
        def _():
            begin = sum(counts[:g])
            block = [ref[...] for ref in pieces[begin : begin + counts[g]]]
            block = block[0] if len(block) == 1 else jnp.concatenate(block, axis=0)
            adjoint_ref[...] = block
            if packs:
                refs[2][0] = block
            half = block.astype(BF16)
            for at, ref in enumerate(coupling_refs):
                place = pl.ds(at * ref.shape[0], ref.shape[0])
                second_ref[place] -= dot(ref[...], half)

    if last:

        @pl.when(u == units - 1)
        def _():
            second = [
                split(second_ref[at * tile : (at + 1) * tile]) for at in range(blocks * parts)
            ]
            for fetch in fetches:
                fetch.wait()
            for block in range(blocks):
                for i in range(parts):
                    held = [
                        split(held_ref[at])
                        for at, place in enumerate(places)
                        if place[:2] == (block, i)
                    ]
                    right = second[block * parts + i : (block + 1) * parts]
                    out_ref[block, i * tile : (i + 1) * tile] = dot(
                        jnp.concatenate([half[part] for part in (0, 1, 0) for half in held], axis=1),
                        jnp.concatenate([half[part] for part in (0, 0, 1) for half in right], axis=0),
                    )


def coupled_step(me, coupling, start, pieces, numbers, adjoint, packs=False, inverse=None):
    depth, count = coupling.shape[0], pieces[0][0].shape[1]
    sub = sum(piece.shape[0] for piece in pieces[0])
    units = len(numbers)

    def unit_of(u):
        unit = numbers[-1]
        for g in range(units - 1):
            unit = jnp.where(u == g, numbers[g], unit)
        return unit

    whole = pl.BlockSpec((depth, count), lambda u, me_ref: (0, 0))
    strip = strip_of(depth)
    strips = depth // strip
    in_specs = [
        pl.BlockSpec(
            (strip, sub), functools.partial(lambda at, u, me_ref: (at, unit_of(u) ^ me_ref[0]), at)
        )
        for at in range(strips)
    ] + [pl.BlockSpec(start.shape, lambda u, me_ref: (0, 0))]
    operands = [coupling] * strips + [start]
    for group in pieces:
        for piece in group:
            in_specs.append(pl.BlockSpec(piece.shape, lambda u, me_ref: (0, 0)))
            operands.append(piece)
    more = {}
    if adjoint is not None:
        in_specs.append(pl.BlockSpec(memory_space=pl.ANY))
        operands.append(adjoint)
        more["input_output_aliases"] = {len(operands): 1}
    flops = 2 * units * depth * sub * count
    moved = units * sub * (2 * depth + 8 * count) + 8 * depth * count
    place = pl.BlockSpec((sub, count), lambda u, me_ref: (unit_of(u) ^ me_ref[0], 0))
    adjoint_shape = jax.ShapeDtypeStruct((coupling.shape[1], count), F32)
    if inverse is None:
        out_specs = [whole, place]
        out_shape = [jax.ShapeDtypeStruct((depth, count), F32), adjoint_shape]
        if packs:
            out_specs.append(pl.BlockSpec((1, sub, count), lambda u, me_ref: (u, 0, 0)))
            out_shape.append(jax.ShapeDtypeStruct((units, sub, count), F32))
        scratch = ()
    else:
        blocks, width, _ = inverse.shape
        tiles = blocks * len(upper_tiles(width // tile_of(width)))
        in_specs.append(pl.BlockSpec(memory_space=pl.ANY))
        operands.append(inverse)
        out_specs = [pl.BlockSpec((blocks, width, count), lambda u, me_ref: (0, 0, 0)), place]
        out_shape = [jax.ShapeDtypeStruct((blocks, width, count), F32), adjoint_shape]
        scratch = (
            pltpu.VMEM((depth, count), F32),
            pltpu.VMEM((tiles, tile_of(width), tile_of(width)), F32),
            pltpu.SemaphoreType.DMA((tiles,)),
        )
        flops += 6 * inverse.size * count
        moved += 4 * inverse.size
    return call(
        functools.partial(
            coupled_kernel,
            tuple(len(group) for group in pieces),
            strips,
            adjoint is not None,
            packs,
            inverse is not None,
        ),
        (units,),
        in_specs,
        out_specs,
        out_shape,
        flops,
        moved,
        scratch=scratch,
        room=48 * MIB,
        **more,
    )(me, *operands)


def on_device(scen_count, col_count, private_seeds, private_inverse, coupling, shared_seed, shared_inverse):
    blocks, width = private_inverse.shape[2:4]
    count = private_seeds.shape[4]
    shard_cols = coupling.shape[3]
    sub = shared_seed.shape[1]
    depth = shared_inverse.shape[4]
    devices = scen_count * col_count
    scen_bits, col_bits = scen_count.bit_length() - 1, col_count.bit_length() - 1

    my_scen, my_col = lax.axis_index("scen"), lax.axis_index("col")
    me_scen = my_scen.astype(jnp.int32).reshape(1)
    me = (my_scen * col_count + my_col).astype(jnp.int32).reshape(1)

    def exchange(array, bit):
        return lax.ppermute(array, AXES, [(w, w ^ (1 << bit)) for w in range(devices)])

    flat_coupling = coupling[0].reshape(blocks * width, shard_cols)
    first, half = first_of(private_seeds[0, 0], private_inverse[0, 0])

    def halved(away, terms, order):
        for step, bit in enumerate(order):
            if step > 0:
                half = terms[-1].shape[0] // 2
                away = sum(term[half : 2 * half] for term in terms)
            terms = terms + [exchange(away, bit)]
        return terms

    core = col_bits
    col_order = list(range(col_bits))
    outer = list(range(core + 1, core + scen_bits))

    orders = [outer, outer[::-1]][: sub // seed_cols(sub)]
    scen_orders = [[bit - core for bit in order] for order in orders]
    arrived = []
    for chunk, order in enumerate(scen_orders):
        away = seed_products(me_scen, flat_coupling, half, sub, [order], 1, chunk * seed_cols(sub))
        arrived.append(exchange(away[0], core))
    own = seed_products(me_scen, flat_coupling, half, sub, scen_orders, 0, 0)
    reduced = reduced_of(
        shared_seed[0],
        [
            [sum(term[:1] for term in terms[:-1]), terms[-1]]
            for terms in (
                halved(sum(term[term.shape[0] // 2 :] for term in pair), list(pair), order)
                for *pair, order in zip(own, arrived, orders)
            )
        ],
    )

    tiles = shared_inverse.reshape(scen_count, *([2] * col_bits), sub, 1, depth)
    orders = [
        outer + col_order,
        outer[1:] + col_order + outer[:1],
        col_order[:1] + outer + col_order[1:],
        outer + col_order,
    ]
    rows = sub // len(orders)

    def products(chunk, base, received=None, earlier=()):
        bits = orders[chunk] if base == 1 << core else orders[chunk][1:]
        return shared_products(
            me, tiles, reduced, bits, base, chunk * rows, rows, received, earlier
        )

    arrived = [exchange(products(chunk, 1 << core), core) for chunk in range(len(orders))]
    away = [
        products(chunk, 1 << order[0], arrived[chunk]) for chunk, order in enumerate(orders)
    ]
    shares = []
    for chunk, order in enumerate(orders):
        kept = products(chunk, 0, earlier=away)
        shares.append(halved(away[chunk], [kept, arrived[chunk]], order))

    near = []
    for part, way in enumerate((outer, outer[::-1])):
        held = {0: share_of(shares[2 * part : 2 * part + 2])}
        for bit in way:
            for number, piece in list(held.items()):
                held[number | (1 << (bit - core))] = exchange(piece, bit)
        near.append(held)
    inverse = private_inverse[0, 0]
    numbers = sorted(near[0])
    middle, last = numbers[1:-1], numbers[-1]
    own = [held[0] for held in near]
    across = [exchange(piece, core) for piece in own]
    far = [[exchange(held[number], core) for held in near] for number in middle]
    second, adjoint = coupled_step(
        me_scen,
        flat_coupling,
        first,
        [own, across] + [[held[number] for held in near] for number in middle],
        [0, 1] + middle,
        None,
    )
    second, adjoint, packed = coupled_step(
        me_scen, flat_coupling, second, [[held[last] for held in near]], [last], adjoint, packs=True
    )
    packed = exchange(packed, core).reshape(sub, count)
    second, adjoint = coupled_step(
        me_scen,
        flat_coupling,
        second,
        far + [[packed]],
        [number | 1 for number in middle + [last]],
        adjoint,
        inverse=inverse,
    )
    return second[None, None], adjoint[None]


def solution(mesh):
    in_specs = (
        P("scen", "col", None, None, None),
        P("scen", "col", None, None, None),
        P("scen", None, None, "col"),
        P("col", "scen", None),
        P(None, None, None, "col", "scen"),
    )
    out_specs = (P("scen", "col", None, None, None), P("col", None, None))
    return jax.shard_map(
        functools.partial(on_device, mesh.shape["scen"], mesh.shape["col"]),
        mesh=mesh,
        in_specs=in_specs,
        out_specs=out_specs,
        check_vma=False,
    )
```

```python
import functools
import math

import jax
import jax.numpy as jnp
from jax import lax
from jax.experimental import pallas as pl
from jax.experimental.pallas import tpu as pltpu
from jax.sharding import PartitionSpec as P

F32, BF16 = jnp.float32, jnp.bfloat16
AXES = ("scen", "col")
MIB = 1024 * 1024


def split(value):
    high = value.astype(BF16)
    return high, (value - high.astype(F32)).astype(BF16)


def dot(left, right):
    return jnp.dot(left, right, preferred_element_type=F32)


def dot3(left, right):
    (left_high, left_low), (right_high, right_low) = left, right
    return dot(left_high, right_high) + (dot(left_low, right_high) + dot(left_high, right_low))


def tile_of(width):
    return 256 if width % 256 == 0 else width


def bytes_of(spec, dtype):
    shape = spec.block_shape
    return 0 if shape is None else math.prod(shape) * dtype.itemsize


def call(kernel, grid, in_specs, out_specs, out_shape, flops, moved, prefetch=1, scratch=(), room=None, earlier=(), **more):
    inputs = prefetch + len(in_specs)
    body = kernel
    if earlier:
        body = lambda *refs: kernel(*refs[:inputs], *refs[inputs + len(earlier) :])
    in_specs = list(in_specs) + [pl.BlockSpec(memory_space=pl.ANY)] * len(earlier)

    def run(*operands):
        operands += tuple(earlier)
        outs = out_shape if isinstance(out_shape, (list, tuple)) else [out_shape]
        specs = out_specs if isinstance(out_specs, (list, tuple)) else [out_specs]
        need = sum(2 * bytes_of(s, o.dtype) for s, o in zip(in_specs, operands[prefetch:]))
        need += sum(2 * bytes_of(s, o.dtype) for s, o in zip(specs, outs))
        need += sum(
            math.prod(s.shape) * jnp.dtype(s.dtype).itemsize for s in scratch if len(s.shape) > 1
        )
        return pl.pallas_call(
            body,
            grid_spec=pltpu.PrefetchScalarGridSpec(
                num_scalar_prefetch=prefetch,
                grid=grid,
                in_specs=in_specs,
                out_specs=out_specs,
                scratch_shapes=list(scratch),
            ),
            out_shape=out_shape,
            compiler_params=pltpu.CompilerParams(vmem_limit_bytes=room or need + 10 * MIB),
            cost_estimate=pl.CostEstimate(
                flops=int(flops) // 1, bytes_accessed=int(moved) // 1, transcendentals=0
            ),
            **more,
        )(*operands)

    return run


def spread(bits, place):
    unit = 0
    for j, bit in enumerate(bits):
        unit = unit | (((place >> (len(bits) - 1 - j)) & 1) << bit)
    return unit


def place_of(bits, unit):
    place = 0
    for bit in bits:
        place = place * 2 + ((unit >> bit) & 1)
    return place


def upper_tiles(count):
    return [(i, j) for i in range(count) for j in range(i, count)]


def first_kernel(parts, *refs):
    seeds_refs, inverse_refs, (first_ref, half_ref) = refs[:parts], refs[parts:-2], refs[-2:]
    tile = seeds_refs[0].shape[1]
    seeds = [split(ref[0].T) for ref in seeds_refs]
    firsts = [None] * parts
    for (i, j), ref in zip(upper_tiles(parts), inverse_refs):
        term = dot3(seeds[i], split(ref[0]))
        firsts[j] = term if i == 0 else firsts[j] + term
    for j, first in enumerate(firsts):
        first_ref[:, j * tile : (j + 1) * tile] = first
        half_ref[:, j * tile : (j + 1) * tile] = first.astype(BF16)


def first_of(seeds, inverse):
    blocks, width, count = seeds.shape
    tile = tile_of(width)
    parts = width // tile
    across = pl.BlockSpec((count, width), lambda b: (0, b))
    return call(
        functools.partial(first_kernel, parts),
        (blocks,),
        [
            pl.BlockSpec((1, tile, count), functools.partial(lambda i, b: (b, i, 0), i))
            for i in range(parts)
        ]
        + [
            pl.BlockSpec((1, tile, tile), functools.partial(lambda i, j, b: (b, i, j), i, j))
            for i, j in upper_tiles(parts)
        ],
        [across, across],
        [
            jax.ShapeDtypeStruct((count, blocks * width), F32),
            jax.ShapeDtypeStruct((count, blocks * width), BF16),
        ],
        6 * blocks * width * width * count,
        4 * blocks * width * (width + 3 * count),
        prefetch=0,
        room=58 * MIB,
    )(*([seeds] * parts), *([inverse] * len(upper_tiles(parts))))


def seed_kernel(pair, strips, orders, base, me_ref, *refs):
    coupling_refs, half_ref = refs[: pair * strips], refs[pair * strips]
    sum_refs = refs[pair * strips + 1 :]
    depth = coupling_refs[0].shape[0]
    cols = sum_refs[0].shape[2]
    for g in range(pair):
        unit = spread(orders[0], pl.program_id(0) * pair + g)
        total = sum(
            dot(half_ref[:, at * depth : (at + 1) * depth], coupling_refs[g * strips + at][...])
            for at in range(strips)
        )
        for chunk, (order, ref) in enumerate(zip(orders, sum_refs)):
            ref[place_of(order, unit)] = total[:, chunk * cols : (chunk + 1) * cols]


def seed_products(me, coupling, half, sub, orders, base, offset):
    count, depth = half.shape
    cols = seed_cols(sub)
    wide = cols * len(orders)
    units = 1 << len(orders[0])
    pair = min(units, 2)
    strip = strip_of(depth)
    strips = depth // strip

    def place(g, strip, f, me_ref):
        unit = spread(orders[0], f * pair + g) | base
        return strip, ((unit ^ me_ref[0]) * sub + offset) // wide

    return call(
        functools.partial(seed_kernel, pair, strips, orders, base),
        (units // pair,),
        [
            pl.BlockSpec((strip, wide), functools.partial(place, g, number))
            for g in range(pair)
            for number in range(strips)
        ]
        + [pl.BlockSpec((count, depth), lambda f, me_ref: (0, 0))],
        [pl.BlockSpec((units, count, cols), lambda f, me_ref: (0, 0, 0))] * len(orders),
        [jax.ShapeDtypeStruct((units, count, cols), F32)] * len(orders),
        2 * units * depth * wide * count,
        units * wide * (2 * depth + 4 * count),
        room=52 * MIB,
    )(me, *([coupling] * (pair * strips)), half)


def strip_of(depth):
    return 256 if depth % 256 == 0 else depth


def seed_cols(sub):
    return sub // 2 if sub % 256 == 0 else sub


def reduced_kernel(chunks, seed_ref, *refs):
    *terms, out_ref = refs
    each = len(terms) // chunks
    cols = terms[0].shape[2]
    for chunk in range(chunks):
        place = pl.ds(chunk * cols, cols)
        total = sum(ref[0] for ref in terms[chunk * each : (chunk + 1) * each])
        out_ref[place] = seed_ref[place] - total.T


def reduced_of(seed, terms):
    whole = pl.BlockSpec(seed.shape, lambda i: (0, 0))
    flat = [term for chunk in terms for term in chunk]
    return call(
        functools.partial(reduced_kernel, len(terms)),
        (1,),
        [whole] + [pl.BlockSpec((1, *term.shape[1:]), lambda i: (0, 0, 0)) for term in flat],
        whole,
        jax.ShapeDtypeStruct(seed.shape, F32),
        0,
        16 * seed.size,
        prefetch=0,
    )(seed, *flat)


def share_kernel(chunks, *refs):
    *terms, out_ref = refs
    each = len(terms) // chunks
    rows = terms[0].shape[1]
    for chunk in range(chunks):
        out_ref[chunk * rows : (chunk + 1) * rows] = sum(
            ref[0] for ref in terms[chunk * each : (chunk + 1) * each]
        )


def share_of(terms):
    _, rows, count = terms[0][0].shape
    flat = [term for chunk in terms for term in chunk]
    shape = (len(terms) * rows, count)
    return call(
        functools.partial(share_kernel, len(terms)),
        (1,),
        [pl.BlockSpec((1, rows, count), lambda i: (0, 0, 0)) for _ in flat],
        pl.BlockSpec(shape, lambda i: (0, 0)),
        jax.ShapeDtypeStruct(shape, F32),
        0,
        4 * rows * count * (len(flat) + len(terms)),
        prefetch=0,
    )(*flat)


def shared_kernel(bits, inner, several, pieces, me_ref, *refs):
    tiles, refs = refs[: several * pieces], refs[several * pieces :]
    seed_ref, *received, out_ref, parts_ref, seed_parts_ref = refs
    depth = seed_ref.shape[0]
    group = 1 << len(inner)
    rows = parts_ref.shape[0] // (group * several)
    lanes = depth // pieces
    step = pl.program_id(0)

    @pl.when(step == 0)
    def _():
        high, low = split(seed_ref[...])
        seed_parts_ref[:depth] = high
        seed_parts_ref[depth : 2 * depth] = high
        seed_parts_ref[2 * depth :] = low

    for number, ref in enumerate(tiles):
        high, low = split(ref.reshape(group * rows, lanes)[...])
        at, place = number % pieces * lanes, pl.ds(number // pieces * group * rows, group * rows)
        parts_ref[place, at : at + lanes] = high
        parts_ref[place, depth + at : depth + at + lanes] = low
        parts_ref[place, 2 * depth + at : 2 * depth + at + lanes] = high
    total = dot(parts_ref[...], seed_parts_ref[...])
    outer_bits = [bit for bit in bits if bit not in inner]
    for g in range(several * group):
        col = spread(inner, g % group) ^ (me_ref[0] & spread(inner, group - 1))
        unit = spread(outer_bits, step * several + g // group) | col
        place = place_of(bits, unit) % out_ref.shape[0]
        term = total[g * rows : (g + 1) * rows]
        if received:
            term = term + received[0][place]
        out_ref[place] = term


def shared_products(me, tiles, seed, bits, base, offset, rows, received=None, earlier=()):
    depth, count = seed.shape
    lanes = min(depth, 128)
    pieces = depth // lanes
    col_bits = tiles.ndim - 4
    units = 1 << len(bits)
    inner = sorted([bit for bit in bits if bit < col_bits], reverse=True)
    outer_bits = [bit for bit in bits if bit >= col_bits]
    group = 1 << len(inner)
    several = 1
    together = int(sorted(bits[len(outer_bits) :], reverse=True) == inner)
    held = group if together else units

    def place(number, piece, f, me_ref):
        unit = (spread(outer_bits, f * several + number) | base) ^ me_ref[0]
        cols = [0 if bit in inner else (unit >> bit) & 1 for bit in reversed(range(col_bits))]
        return (unit >> col_bits, *cols, offset // rows, 0, piece)

    block = [2 if bit in inner else 1 for bit in reversed(range(col_bits))]
    in_specs = [
        pl.BlockSpec((1, *block, rows, 1, lanes), functools.partial(place, number, piece))
        for number in range(several)
        for piece in range(pieces)
    ] + [pl.BlockSpec((depth, count), lambda f, me_ref: (0, 0))]
    operands = [tiles] * (several * pieces) + [seed]
    if received is not None:
        skip = (received.shape[0] - units) // held
        in_specs.append(
            pl.BlockSpec((held, rows, count), lambda f, me_ref: (skip + f * together, 0, 0))
        )
        operands.append(received)
    return call(
        functools.partial(shared_kernel, bits, inner, several, pieces),
        (units // (group * several),),
        in_specs,
        pl.BlockSpec((held, rows, count), lambda f, me_ref: (f * together, 0, 0)),
        jax.ShapeDtypeStruct((units, rows, count), F32),
        6 * units * rows * depth * count,
        4 * units * rows * (depth + count),
        scratch=[
            pltpu.VMEM((several * group * rows, 3 * depth), BF16),
            pltpu.VMEM((3 * depth, count), BF16),
        ],
        room=34 * MIB,
        earlier=earlier,
    )(me, *operands)


def coupled_kernel(counts, strips, aliased, packs, last, me_ref, *refs):
    coupling_refs, start_ref, refs = refs[:strips], refs[strips], refs[strips + 1 :]
    units, given = len(counts), sum(counts)
    pieces, refs = refs[:given], refs[given:]
    refs = refs[1:] if aliased else refs
    u = pl.program_id(0)
    if last:
        inverse_ref, out_ref, adjoint_ref, second_ref, held_ref, sems = refs
        blocks, width, _ = inverse_ref.shape
        tile = held_ref.shape[2]
        parts = width // tile
        places = [(block, i, j) for block in range(blocks) for i, j in upper_tiles(parts)]
        fetches = [
            pltpu.make_async_copy(
                inverse_ref.at[block, pl.ds(i * tile, tile), pl.ds(j * tile, tile)],
                held_ref.at[at],
                sems.at[at],
            )
            for at, (block, i, j) in enumerate(places)
        ]
    else:
        second_ref, adjoint_ref = refs[:2]

    @pl.when(u == 0)
    def _():
        if last:
            for fetch in fetches:
                fetch.start()
        second_ref[...] = start_ref[...] if aliased else start_ref[...].T

    for g in range(units):

        @pl.when(u == g)
        def _():
            begin = sum(counts[:g])
            block = [ref[...] for ref in pieces[begin : begin + counts[g]]]
            block = block[0] if len(block) == 1 else jnp.concatenate(block, axis=0)
            adjoint_ref[...] = block
            if packs:
                refs[2][0] = block
            half = block.astype(BF16)
            for at, ref in enumerate(coupling_refs):
                place = pl.ds(at * ref.shape[0], ref.shape[0])
                second_ref[place] -= dot(ref[...], half)

    if last:

        @pl.when(u == units - 1)
        def _():
            second = [
                split(second_ref[at * tile : (at + 1) * tile]) for at in range(blocks * parts)
            ]
            for fetch in fetches:
                fetch.wait()
            for block in range(blocks):
                for i in range(parts):
                    held = [
                        split(held_ref[at])
                        for at, place in enumerate(places)
                        if place[:2] == (block, i)
                    ]
                    right = second[block * parts + i : (block + 1) * parts]
                    out_ref[block, i * tile : (i + 1) * tile] = dot(
                        jnp.concatenate([half[part] for part in (0, 1, 0) for half in held], axis=1),
                        jnp.concatenate([half[part] for part in (0, 0, 1) for half in right], axis=0),
                    )


def coupled_step(me, coupling, start, pieces, numbers, adjoint, packs=False, inverse=None):
    depth, count = coupling.shape[0], pieces[0][0].shape[1]
    sub = sum(piece.shape[0] for piece in pieces[0])
    units = len(numbers)

    def unit_of(u):
        unit = numbers[-1]
        for g in range(units - 1):
            unit = jnp.where(u == g, numbers[g], unit)
        return unit

    whole = pl.BlockSpec((depth, count), lambda u, me_ref: (0, 0))
    strip = strip_of(depth)
    strips = depth // strip
    in_specs = [
        pl.BlockSpec(
            (strip, sub), functools.partial(lambda at, u, me_ref: (at, unit_of(u) ^ me_ref[0]), at)
        )
        for at in range(strips)
    ] + [pl.BlockSpec(start.shape, lambda u, me_ref: (0, 0))]
    operands = [coupling] * strips + [start]
    for group in pieces:
        for piece in group:
            in_specs.append(pl.BlockSpec(piece.shape, lambda u, me_ref: (0, 0)))
            operands.append(piece)
    more = {}
    if adjoint is not None:
        in_specs.append(pl.BlockSpec(memory_space=pl.ANY))
        operands.append(adjoint)
        more["input_output_aliases"] = {len(operands): 1}
    flops = 2 * units * depth * sub * count
    moved = units * sub * (2 * depth + 8 * count) + 8 * depth * count
    place = pl.BlockSpec((sub, count), lambda u, me_ref: (unit_of(u) ^ me_ref[0], 0))
    adjoint_shape = jax.ShapeDtypeStruct((coupling.shape[1], count), F32)
    if inverse is None:
        out_specs = [whole, place]
        out_shape = [jax.ShapeDtypeStruct((depth, count), F32), adjoint_shape]
        if packs:
            out_specs.append(pl.BlockSpec((1, sub, count), lambda u, me_ref: (u, 0, 0)))
            out_shape.append(jax.ShapeDtypeStruct((units, sub, count), F32))
        scratch = ()
    else:
        blocks, width, _ = inverse.shape
        tiles = blocks * len(upper_tiles(width // tile_of(width)))
        in_specs.append(pl.BlockSpec(memory_space=pl.ANY))
        operands.append(inverse)
        out_specs = [pl.BlockSpec((blocks, width, count), lambda u, me_ref: (0, 0, 0)), place]
        out_shape = [jax.ShapeDtypeStruct((blocks, width, count), F32), adjoint_shape]
        scratch = (
            pltpu.VMEM((depth, count), F32),
            pltpu.VMEM((tiles, tile_of(width), tile_of(width)), F32),
            pltpu.SemaphoreType.DMA((tiles,)),
        )
        flops += 6 * inverse.size * count
        moved += 4 * inverse.size
    return call(
        functools.partial(
            coupled_kernel,
            tuple(len(group) for group in pieces),
            strips,
            adjoint is not None,
            packs,
            inverse is not None,
        ),
        (units,),
        in_specs,
        out_specs,
        out_shape,
        flops,
        moved,
        scratch=scratch,
        room=48 * MIB,
        **more,
    )(me, *operands)


def on_device(scen_count, col_count, private_seeds, private_inverse, coupling, shared_seed, shared_inverse):
    blocks, width = private_inverse.shape[2:4]
    count = private_seeds.shape[4]
    shard_cols = coupling.shape[3]
    sub = shared_seed.shape[1]
    depth = shared_inverse.shape[4]
    devices = scen_count * col_count
    scen_bits, col_bits = scen_count.bit_length() - 1, col_count.bit_length() - 1

    my_scen, my_col = lax.axis_index("scen"), lax.axis_index("col")
    me_scen = my_scen.astype(jnp.int32).reshape(1)
    me = (my_scen * col_count + my_col).astype(jnp.int32).reshape(1)

    def exchange(array, bit):
        return lax.ppermute(array, AXES, [(w, w ^ (1 << bit)) for w in range(devices)])

    flat_coupling = coupling[0].reshape(blocks * width, shard_cols)
    first, half = first_of(private_seeds[0, 0], private_inverse[0, 0])

    def halved(away, terms, order):
        for step, bit in enumerate(order):
            if step > 0:
                half = terms[-1].shape[0] // 2
                away = sum(term[half : 2 * half] for term in terms)
            terms = terms + [exchange(away, bit)]
        return terms

    core = col_bits
    col_order = list(range(col_bits))
    outer = list(range(core + 1, core + scen_bits))

    orders = [outer, outer[::-1]][: sub // seed_cols(sub)]
    scen_orders = [[bit - core for bit in order] for order in orders]
    arrived = []
    for chunk, order in enumerate(scen_orders):
        away = seed_products(me_scen, flat_coupling, half, sub, [order], 1, chunk * seed_cols(sub))
        arrived.append(exchange(away[0], core))
    own = seed_products(me_scen, flat_coupling, half, sub, scen_orders, 0, 0)
    reduced = reduced_of(
        shared_seed[0],
        [
            [sum(term[:1] for term in terms[:-1]), terms[-1]]
            for terms in (
                halved(sum(term[term.shape[0] // 2 :] for term in pair), list(pair), order)
                for *pair, order in zip(own, arrived, orders)
            )
        ],
    )

    tiles = shared_inverse.reshape(scen_count, *([2] * col_bits), sub, 1, depth)
    orders = [
        outer + col_order,
        outer[1:] + col_order + outer[:1],
        col_order[:1] + outer + col_order[1:],
        outer + col_order,
    ]
    rows = sub // len(orders)

    def products(chunk, base, received=None, earlier=()):
        bits = orders[chunk] if base == 1 << core else orders[chunk][1:]
        return shared_products(
            me, tiles, reduced, bits, base, chunk * rows, rows, received, earlier
        )

    arrived = [exchange(products(chunk, 1 << core), core) for chunk in range(len(orders))]
    away = [
        products(chunk, 1 << order[0], arrived[chunk]) for chunk, order in enumerate(orders)
    ]
    shares = []
    for chunk, order in enumerate(orders):
        kept = products(chunk, 0, earlier=away)
        shares.append(halved(away[chunk], [kept, arrived[chunk]], order))

    near = []
    for part, way in enumerate((outer, outer[::-1])):
        held = {0: share_of(shares[2 * part : 2 * part + 2])}
        for bit in way:
            for number, piece in list(held.items()):
                held[number | (1 << (bit - core))] = exchange(piece, bit)
        near.append(held)
    inverse = private_inverse[0, 0]
    numbers = sorted(near[0])
    middle, last = numbers[1:-1], numbers[-1]
    own = [held[0] for held in near]
    across = [exchange(piece, core) for piece in own]
    far = [[exchange(held[number], core) for held in near] for number in middle]
    second, adjoint = coupled_step(
        me_scen,
        flat_coupling,
        first,
        [own, across] + [[held[number] for held in near] for number in middle],
        [0, 1] + middle,
        None,
    )
    second, adjoint, packed = coupled_step(
        me_scen, flat_coupling, second, [[held[last] for held in near]], [last], adjoint, packs=True
    )
    packed = exchange(packed, core).reshape(sub, count)
    second, adjoint = coupled_step(
        me_scen,
        flat_coupling,
        second,
        far + [[packed]],
        [number | 1 for number in middle + [last]],
        adjoint,
        inverse=inverse,
    )
    return second[None, None], adjoint[None]


def solution(mesh):
    in_specs = (
        P("scen", "col", None, None, None),
        P("scen", "col", None, None, None),
        P("scen", None, None, "col"),
        P("col", "scen", None),
        P(None, None, None, "col", "scen"),
    )
    out_specs = (P("scen", "col", None, None, None), P("col", None, None))
    return jax.shard_map(
        functools.partial(on_device, mesh.shape["scen"], mesh.shape["col"]),
        mesh=mesh,
        in_specs=in_specs,
        out_specs=out_specs,
        check_vma=False,
    )
```
